32 devices in a mesh: spatial: 8 (over z, y), dp: 4 (over x, core).
Axes of the slice: x: 2, y: 2, z: 4, core: 2. Of those that a mesh axis runs over, the one named last changes fastest.
Arguments:
- features: bfloat16 [4, 48, 8, 8, 512], P('dp', 'spatial'), may hold values from -6 to 6
- masks: int32 [4, 48, 512], P('dp', 'spatial'), may hold values 0 or 1
- rulebook: int32 [4, 48, 27], P('dp', 'spatial'), may hold values from 0 to 22, as said below
- send_lists: int32 [4, 8, 8, 2], P('dp', 'spatial'), may hold values from 0 to 6, as said below
- conv_weight: bfloat16 [27, 64, 64], replicated, may hold values from -0.15625 to 0.15625
- down_weight: bfloat16 [8, 64, 128], replicated, may hold values from -0.25 to 0.25
- cotangent: bfloat16 [4, 48, 4, 4, 512], P('dp', 'spatial'), may hold values from -6 to 6
Outputs:
- coarse_out: bfloat16 [4, 48, 4, 4, 512], P('dp', 'spatial')
- grad_features: bfloat16 [4, 48, 8, 8, 512], P('dp', 'spatial')
- grad_conv: float32 [27, 64, 64], replicated
- grad_down: float32 [8, 64, 128], replicated
The draws below stay inside these ranges and needn't reach their ends.
Inputs may be any that keep to these rules, and one draw needn't show every extreme that they name: `send_lists`: with q = d // 4, device d of spatial is region ((q % 2) (1) + q // 2, (d // 2) % 2, d % 2) of a 2^3 grid without wrap. A device sends 2 distinct bricks to each region sharing a face with it, one brick (slot 0) to each sharing only an edge or a corner, and nothing to itself or to other regions; empty slots hold 6. Entries index the owning device's extended list; entry 13 of a brick is the brick's own local index; entries name only own bricks, filled received slots and 22, and each of these appears in the device's rulebook.
All inputs are finite; a program needn't handle non-finite values. No bound on the sum of `masks` on one device may be relied on, other than what follows from the above.
Results may differ from the reference program's by a relative error of at most 0.0095.
Values may be sent and summed in bfloat16 or wider, within the bound.
A program may use at most 192 MiB of HBM per device.

```python
import jax
import jax.numpy as jnp
from jax import lax

C = 64
CO = 128
BR = 8
CAP = 2
BD = 6
SCENES = 4
NB = 48
HB = 4
SLOTS = 22
GRID = 2
N_SPATIAL = 8


def slot_counts():
    index = jnp.arange(N_SPATIAL, dtype=jnp.int32)
    slow = index // (GRID * GRID)
    first = slow % 2 * (GRID // 2) + slow // 2
    coords = jnp.stack([first, index // GRID % GRID, index % GRID], axis=1)
    apart = jnp.abs(coords[:, None, :] - coords[None, :, :])
    near = jnp.all(apart <= 1, axis=2)
    moved = jnp.sum((apart > 0).astype(jnp.int32), axis=2)
    counts = jnp.where(moved == 1, CAP, 1)
    return jnp.where(near & (moved > 0), counts, 0).astype(jnp.int32)


def draw_send_lists(key, part):
    scores = jax.random.randint(key, (SCENES, N_SPATIAL, N_SPATIAL, BD), 0, 2 ** 16) * BD + jnp.arange(BD, dtype=jnp.int32)
    order = jnp.argsort(scores, axis=-1, stable=True)[..., :CAP].astype(jnp.int32)
    counts = slot_counts()
    used = jnp.arange(CAP, dtype=jnp.int32)[None, None, None, :] < counts[None, :, :, None]
    return jnp.where(used, order, BD).astype(jnp.int32)


def draw_rulebook(key, part):
    span = SLOTS + 1
    total = 26 * BD
    extra = total - span
    groups = SCENES * N_SPATIAL
    key_pick, key_fill, key_empty, key_order = jax.random.split(jax.random.fold_in(key, 7), 4)
    counts = slot_counts()
    slot_used = jnp.arange(CAP, dtype=jnp.int32)[None, None, :] < counts[:, :, None]
    received = jnp.transpose(slot_used, (1, 0, 2)).reshape(N_SPATIAL, N_SPATIAL * CAP)
    valid = jnp.concatenate([jnp.ones((N_SPATIAL, BD), bool), received, jnp.ones((N_SPATIAL, 1), bool)], axis=1)
    sort_key = jnp.where(valid, 0, 1).astype(jnp.int32) * span + jnp.arange(span, dtype=jnp.int32)
    ordered = jnp.argsort(sort_key, axis=1, stable=True).astype(jnp.int32)
    number = jnp.sum(valid.astype(jnp.int32), axis=1)
    ordered = jnp.tile(ordered, (SCENES, 1))
    number = jnp.tile(number, (SCENES,))[:, None]
    fill_pick = jax.random.randint(key_fill, (groups, span), 0, 2 ** 16) % number
    position = jnp.arange(span, dtype=jnp.int32)[None, :]
    base_pos = jnp.where(position < number, position, fill_pick).astype(jnp.int32)
    base = jnp.take_along_axis(ordered, base_pos, axis=1)
    pick_pos = (jax.random.randint(key_pick, (groups, extra), 0, 2 ** 16) % number).astype(jnp.int32)
    picked = jnp.take_along_axis(ordered, pick_pos, axis=1)
    empty = jax.random.randint(key_empty, (groups, extra), 0, 3) == 0
    tail = jnp.where(empty, SLOTS, picked).astype(jnp.int32)
    entries = jnp.concatenate([base, tail], axis=1)
    scores = jax.random.randint(key_order, (groups, total), 0, 2 ** 16) * total + jnp.arange(total, dtype=jnp.int32)
    order = jnp.argsort(scores, axis=-1, stable=True)
    mixed = jnp.take_along_axis(entries, order, axis=1).reshape(groups, BD, 26)
    centre = jnp.broadcast_to(jnp.arange(BD, dtype=jnp.int32)[None, :, None], (groups, BD, 1))
    full = jnp.concatenate([mixed[:, :, :13], centre, mixed[:, :, 13:]], axis=2)
    return full.reshape(SCENES, NB, 27).astype(jnp.int32)


def touch_ends(array, rng, smallest, top_value):
    longest = array.shape.index(max(array.shape))
    spots = []
    for shift in (0, 1):
        where = [jax.random.randint(jax.random.fold_in(rng, axis), (), 0, length) for axis, length in enumerate(array.shape)]
        where[longest] = (where[longest] + shift) % array.shape[longest]
        spots.append(tuple(where))
    return array.at[spots[0]].set(smallest).at[spots[1]].set(top_value)


def levels(own_key, shape, cuts, low, top_value):
    gain, own = 1.0, jax.random.fold_in(own_key, 6)
    for dim, blocks in cuts:
        steps = jnp.exp(jax.random.uniform(jax.random.fold_in(own, dim), (blocks,), jnp.float32, low / len(cuts), top_value / len(cuts)))
        gain = gain * jnp.repeat(steps, shape[dim] // blocks).reshape([-1 if axis == dim else 1 for axis in range(len(shape))])
    return gain


def normal_values(rng, shape, deviation, most, cuts=(), kind=jnp.bfloat16):
    values = jax.random.normal(rng, shape, jnp.float32) * deviation
    if len(cuts) > 0:
        values = levels(rng, shape, cuts, -0.22, 0.18) * values
    return jnp.clip(values, min=-most, max=most).astype(kind)


def setup_inputs(seed: int = 0) -> dict:
    seeds = jax.random.split(jax.random.key(seed), 8)
    features = normal_values(seeds[0], (SCENES, NB, BR, BR, BR * C), 1.0, 6.0, ((0, 4), (1, 8)))
    masks = touch_ends((jax.random.randint(seeds[1], (SCENES, NB, BR**3), 0, 5) < 2).astype(jnp.int32), jax.random.fold_in(seeds[1], 1), 0, 1)
    rulebook = draw_rulebook(jax.random.fold_in(seeds[7], 71), 0)
    send_lists = draw_send_lists(jax.random.fold_in(seeds[7], 71), 0)
    conv_weight = normal_values(seeds[4], (27, C, C), (27 * C) ** -0.5, 0.15625)
    down_weight = normal_values(seeds[5], (8, C, CO), (8 * C) ** -0.5, 0.25)
    cotangent = normal_values(seeds[6], (SCENES, NB, HB, HB, HB * CO), 1.0, 6.0, ((0, 4), (1, 8)))
    return dict(features=features, masks=masks, rulebook=rulebook, send_lists=send_lists, conv_weight=conv_weight, down_weight=down_weight, cotangent=cotangent)


def rim_range(pos, edge):
    if pos == 0:
        return (edge - 1, edge)
    if pos == 1:
        return (0, edge)
    return (0, 1)

def assemble(extended, table, edge, width):
    planes = []
    for x_pos in range(3):
        rows = []
        for y_pos in range(3):
            cols = []
            for z_pos in range(3):
                x_lo, x_hi = rim_range(x_pos, edge)
                y_lo, y_hi = rim_range(y_pos, edge)
                z_lo, z_hi = rim_range(z_pos, edge)
                part = extended[:, x_lo:x_hi, y_lo:y_hi, z_lo * width:z_hi * width]
                cols.append(jnp.take(part, table[:, x_pos * 9 + y_pos * 3 + z_pos], axis=0))
            rows.append(jnp.concatenate(cols, axis=3))
        planes.append(jnp.concatenate(rows, axis=2))
    return jnp.concatenate(planes, axis=1)

def conv_split(padded, weights, edge, width):
    count = padded.shape[0]
    blocks = padded.reshape(count, edge + 2, edge + 2, edge + 2, width)
    total = jnp.zeros((count, edge, edge, edge, width), jnp.float32)
    for x_pos in range(3):
        for y_pos in range(3):
            for z_pos in range(3):
                piece = blocks[:, x_pos:x_pos + edge, y_pos:y_pos + edge, z_pos:z_pos + edge]
                total = total + jnp.einsum('nxyzi,io->nxyzo', piece, weights[x_pos * 9 + y_pos * 3 + z_pos])
    return total.reshape(count, edge, edge, edge * width)

def silu_grad(value):
    sig = jax.nn.sigmoid(value)
    return sig * (1.0 + value * (1.0 - sig))

def to_children(hidden, count, half, width):
    split = hidden.reshape(count, half, 2, half, 2, half, 2 * width)
    return split.transpose(0, 1, 3, 5, 2, 4, 6).reshape(count * half ** 3, 8 * width)

def from_children(grads, count, half, width):
    split = grads.reshape(count, half, half, half, 2, 2, 2 * width)
    return split.transpose(0, 1, 4, 2, 5, 3, 6).reshape(count, 2 * half, 2 * half, 2 * half * width)

def reference(features, masks, rulebook, send_lists, conv_weight, down_weight, cotangent):
    edge, width, half, peers, count, slots = (BR, C, HB, N_SPATIAL, BD, CAP)
    conv32 = conv_weight.astype(jnp.float32)
    flat_down = down_weight.reshape(8 * width, CO)
    scale = float(SCENES * NB * BR ** 3) ** (-0.5)
    conv_total = jnp.zeros((27, width, width), jnp.float32)
    down_total = jnp.zeros((8 * width, CO), jnp.float32)
    outputs = []
    grad_list = []
    for scene in range(SCENES):
        voxels = masks[scene].reshape(peers, count, edge, edge, edge)
        keep = jnp.repeat(voxels, width, axis=4).astype(jnp.bfloat16)
        masked = features[scene].reshape(peers, count, edge, edge, edge * width) * keep
        masked_ext = jnp.concatenate([masked, jnp.zeros((peers, 1, edge, edge, edge * width), jnp.bfloat16)], axis=1)
        tables = rulebook[scene].reshape(peers, count, 27)
        coarse_all = voxels.reshape(peers, count, half, 2, half, 2, half, 2).max(axis=(3, 5, 7))
        cot_all = cotangent[scene].reshape(peers, count * half ** 3, CO)
        sends = send_lists[scene]
        owners = jnp.arange(peers).astype(jnp.int32)[:, None]

        def device_step(carry, device):
            grads, conv_acc, down_acc = carry
            chosen = sends[:, device, :]
            arrived = masked_ext[owners, chosen].reshape(peers * slots, edge, edge, edge * width)
            extended = jnp.concatenate([masked[device], arrived, jnp.zeros((1, edge, edge, edge * width), jnp.bfloat16)], axis=0)
            table = tables[device]
            keep32 = keep[device].astype(jnp.float32)

            def hidden_map(ext32, weight32):
                return conv_split(assemble(ext32, table, edge, width), weight32, edge, width)
            raw, pullback = jax.vjp(hidden_map, extended.astype(jnp.float32), conv32)
            pre_hidden = raw * keep32
            hidden = jax.nn.silu(pre_hidden).astype(jnp.bfloat16)
            children = to_children(hidden, count, half, width)
            pre_out = jnp.dot(children, flat_down, preferred_element_type=jnp.float32)
            coarse = coarse_all[device].reshape(-1, 1).astype(jnp.float32)
            output = (jax.nn.silu(pre_out) * coarse).astype(jnp.bfloat16)
            grad_pre = (cot_all[device].astype(jnp.float32) * coarse * silu_grad(pre_out)).astype(jnp.bfloat16)
            down_part = jnp.dot(children.T, grad_pre, preferred_element_type=jnp.float32)
            grad_children = jnp.dot(grad_pre, flat_down.T, preferred_element_type=jnp.float32)
            grad_hidden = from_children(grad_children, count, half, width)
            grad_pre_hidden = (grad_hidden * silu_grad(pre_hidden) * keep32).astype(jnp.bfloat16)
            grad_ext, conv_part = pullback(grad_pre_hidden.astype(jnp.float32))
            returning = lax.optimization_barrier(grad_ext[count:count + peers * slots].astype(jnp.bfloat16))
            returning = returning.astype(jnp.float32).reshape(peers, slots, edge, edge, edge * width)
            grads = grads.at[device, :count].add(grad_ext[:count])
            grads = grads.at[owners, chosen].add(returning)
            return ((grads, conv_acc + conv_part, down_acc + down_part), output.reshape(count, half, half, half * CO))
        start = (jnp.zeros((peers, count + 1, edge, edge, edge * width), jnp.float32), conv_total, down_total)
        (grads, conv_total, down_total), output = lax.scan(device_step, start, jnp.arange(peers).astype(jnp.int32))
        grads = grads[:, :count]
        outputs.append(output.reshape(NB, half, half, half * CO))
        grad_list.append((grads * keep.astype(jnp.float32)).astype(jnp.bfloat16).reshape(NB, edge, edge, edge * width))
    coarse_out = jnp.stack(outputs, axis=0)
    grad_features = jnp.stack(grad_list, axis=0)
    grad_conv = conv_total * scale
    grad_down = down_total.reshape(8, width, CO) * scale
    return (coarse_out, grad_features, grad_conv, grad_down)
```

```python
import functools

import jax
import jax.numpy as jnp
from jax import lax
from jax.experimental import pallas as pl
from jax.experimental.pallas import tpu as pltpu
from jax.sharding import PartitionSpec as P

F32 = jnp.float32
BF16 = jnp.bfloat16
VMEM_BYTES = 56 * 1024 * 1024


def silu_grad(value):
    sig = jax.nn.sigmoid(value)
    return sig * (1.0 + value * (1.0 - sig))


def first_kernel(chosen, feats, mask, masked, keepx, outgoing):
    count = feats.shape[0]
    slots = outgoing.shape[0]
    vox = lax.broadcasted_iota(jnp.int32, (64, 512), 1)
    row = lax.broadcasted_iota(jnp.int32, (64, 512), 0)
    own_row = (vox // 8) == row
    v_index = lax.broadcasted_iota(jnp.int32, (512, 512), 0)
    l_index = lax.broadcasted_iota(jnp.int32, (512, 512), 1)
    spread = ((v_index % 8) == (l_index // 64)).astype(F32).astype(BF16)
    for b in range(count):
        picked = jnp.where(own_row, mask[b : b + 1, :].astype(F32), 0.0).astype(BF16)
        keep = jnp.dot(picked, spread, preferred_element_type=F32)
        keepx[b] = keep.astype(BF16)
        masked[b] = (feats[b].astype(F32) * keep).astype(BF16)
    masked[count] = jnp.zeros((64, 512), BF16)

    def send(s, carry):
        outgoing[s] = masked[chosen[s]]
        return carry

    lax.fori_loop(0, slots, send, 0)


def main_kernel(
    table, masked, arrived, keepx, weight, down, cot,
    out, own, ret, wgrad,
    ext, gext, lhs, asm, dpad, pre, hid, keep, grad, grad_t, wpair, sems,
):
    count = keepx.shape[0]
    slots = arrived.shape[0]
    total = ext.shape[0]
    half_rows = count * 128
    rows = 2 * half_rows
    lane = lax.broadcasted_iota(jnp.int32, (8, 128), 1)

    fetch_own = pltpu.make_async_copy(masked.at[pl.ds(0, count)], ext.at[pl.ds(0, count)], sems.at[0])
    fetch_rest = pltpu.make_async_copy(arrived, ext.at[pl.ds(count, slots)], sems.at[1])
    fetch_own.start()
    fetch_rest.start()
    ext[total - 1] = jnp.zeros((64, 512), BF16)

    def clear(e, carry):
        gext[e] = jnp.zeros((64, 512), F32)
        return carry

    lax.fori_loop(0, total, clear, 0)

    for tap in range(9):
        taps = weight[tap * 192 : tap * 192 + 192, :].astype(F32)
        zero = jnp.zeros((64, 64), F32)
        left = jnp.concatenate([taps, zero], axis=0)
        right = jnp.concatenate([zero, taps], axis=0)
        wpair[tap * 256 : tap * 256 + 256, :] = jnp.concatenate([left, right], axis=1).astype(BF16)
    fetch_own.wait()
    fetch_rest.wait()

    def gather_brick(b, carry):
        for y_pos in range(3):
            for x_pos in range(3):
                src = ((48, 64), (0, 64), (0, 16))[x_pos]
                cut = ((8, 16), (0, 64), (0, 8))[x_pos]
                dst = ((0, 1), (1, 9), (9, 10))[x_pos]
                tiles = (dst[1] - dst[0], 8, 128)
                low = lax.broadcasted_iota(jnp.int32, tiles, 2) < 64
                base = x_pos * 9 + y_pos * 3

                def load(index, lo):
                    part = ext[index, src[0] : src[1], lo : lo + 128].astype(F32)
                    part = pltpu.roll(part[cut[0] : cut[1]], 64, 1)
                    return part.reshape(tiles)

                pieces = [load(table[b, base], 384)]
                mid = table[b, base + 1]
                for j in range(4):
                    pieces.append(load(mid, 128 * j))
                pieces.append(load(table[b, base + 2], 0))
                for k in range(5):
                    asm[y_pos, dst[0] : dst[1], :, 128 * k : 128 * k + 128] = jnp.where(
                        low, pieces[k], pieces[k + 1]
                    )
        sub = lax.broadcasted_iota(jnp.int32, (10, 8, 128), 1)
        for k in range(5):
            at = slice(128 * k, 128 * k + 128)
            mid = asm[1, :, :, at]
            below = pltpu.roll(jnp.where(sub == 7, asm[0, :, :, at], mid), 1, 1)
            above = pltpu.roll(jnp.where(sub == 0, asm[2, :, :, at], mid), 7, 1)
            for dy, value in enumerate((below, mid, above)):
                split = value.reshape(5, 2, 8, 128)
                for dx in range(3):
                    tap = dx * 3 + dy
                    for ox in range(2):
                        start, parity = (dx + ox) // 2, (dx + ox) % 2
                        block = split[start : start + 4, parity].reshape(32, 128).astype(BF16)
                        for p, part in ((k, 0), (k - 1, 1)):
                            if 0 <= p < 4:
                                at_row = pl.multiple_of(ox * half_rows + b * 128 + p * 32, 32)
                                col = tap * 256 + part * 128
                                lhs[pl.ds(at_row, 32), col : col + 128] = block
        spread = keepx[b].astype(F32).reshape(4, 2, 8, 512)
        for ox in range(2):
            for p in range(4):
                at_row = pl.multiple_of(ox * half_rows + b * 128 + p * 32, 32)
                keep[pl.ds(at_row, 32), :] = spread[:, ox, :, 128 * p : 128 * p + 128].reshape(32, 128)
        return carry

    lax.fori_loop(0, count, gather_brick, 0)

    def forward(i, carry):
        at = pl.ds(pl.multiple_of(i * 256, 256), 256)
        value = jnp.dot(lhs[at, :], wpair[...], preferred_element_type=F32) * keep[at, :]
        pre[at, :] = value
        hid[at, :] = value * jax.nn.sigmoid(value)
        return carry

    lax.fori_loop(0, count, forward, 0)

    coarse_rows = count * 64
    child = []
    summed = None
    coarse = None
    for o in range(4):
        at = pl.ds((o // 2) * half_rows + o % 2, coarse_rows, stride=2)
        child.append(hid[at, :].astype(BF16))
        term = jnp.dot(child[o], down[o * 128 : o * 128 + 128, :], preferred_element_type=F32)
        summed = term if o == 0 else summed + term
        active = keep[at, :]
        coarse = active if o == 0 else jnp.maximum(coarse, active)
    coarse = jnp.maximum(coarse, pltpu.roll(coarse, 64, 1))
    sig = jax.nn.sigmoid(summed)
    result = (summed * sig * coarse).astype(BF16)
    cots = []
    for b in range(count):
        for p in range(4):
            lo = (b * 4 + p) * 16
            out[b, :, 128 * p : 128 * p + 128] = result[lo : lo + 16, :]
            cots.append(cot[b, :, 128 * p : 128 * p + 128])
    upstream = jnp.concatenate(cots, axis=0).astype(F32)
    grad_pre = (upstream * coarse * (sig * (1.0 + summed * (1.0 - sig)))).astype(BF16)
    for o in range(4):
        part = lax.dot_general(
            child[o], grad_pre, (((0,), (0,)), ((), ())), preferred_element_type=F32
        )
        wgrad[896 + o * 128 : 896 + o * 128 + 128, :] = part.astype(BF16)
        back = lax.dot_general(
            grad_pre,
            down[o * 128 : o * 128 + 128, :],
            (((1,), (1,)), ((), ())),
            preferred_element_type=F32,
        )
        hid[pl.ds((o // 2) * half_rows + o % 2, coarse_rows, stride=2), :] = back
    if wgrad.shape[0] > 1408:
        wgrad[1408:, :] = jnp.zeros((wgrad.shape[0] - 1408, 128), BF16)

    def hidden_grad(i, carry):
        at = pl.ds(pl.multiple_of(i * 256, 256), 256)
        value = hid[at, :] * silu_grad(pre[at, :]) * keep[at, :]
        grad[at, :] = value.astype(BF16)
        grad_t[:, at] = value.T.astype(BF16)
        return carry

    lax.fori_loop(0, count, hidden_grad, 0)

    wide = lax.broadcasted_iota(jnp.int32, (64, 128), 1)
    spare = None
    for tap in range(9):
        both = jnp.dot(
            grad_t[...], lhs[:, tap * 256 : tap * 256 + 256], preferred_element_type=F32
        )
        sums = both[0:64, :] + pltpu.roll(both[64:128, :], 192, 1)
        wgrad[tap * 64 : tap * 64 + 64, :] = sums[:, 0:128].astype(BF16)
        last = sums[:, 128:256]
        if tap % 2 == 0:
            spare = last
        if tap % 2 == 1 or tap == 8:
            other = pltpu.roll(last, 64, 1) if tap % 2 == 1 else jnp.zeros_like(last)
            lo = 576 + (tap // 2) * 64
            wgrad[lo : lo + 64, :] = jnp.where(wide < 64, spare, other).astype(BF16)

    def spread_brick(b, carry):
        low_rows = pl.multiple_of(b * 128, 128)
        for ox in range(2):
            dpad[ox * 128 : ox * 128 + 128, :] = lax.dot_general(
                grad[pl.ds(ox * half_rows + low_rows, 128), :],
                wpair[...],
                (((1,), (1,)), ((), ())),
                preferred_element_type=F32,
            )
        sub = lax.broadcasted_iota(jnp.int32, (8, 128), 0)
        for xp in range(10):
            for k in range(5):
                acc = [None, None, None]
                for dy in range(3):
                    for dx in range(3):
                        x = xp - dx
                        if not 0 <= x < 8:
                            continue
                        for p, part in ((k, 0), (k - 1, 1)):
                            if 0 <= p < 4:
                                at_row = (x % 2) * 128 + p * 32 + (x // 2) * 8
                                col = (dx * 3 + dy) * 256 + part * 128
                                tile = dpad[at_row : at_row + 8, col : col + 128]
                                acc[dy] = tile if acc[dy] is None else acc[dy] + tile
                below = pltpu.roll(acc[0], 7, 0)
                above = pltpu.roll(acc[2], 1, 0)
                mid = acc[1] + jnp.where(sub < 7, below, 0.0) + jnp.where(sub > 0, above, 0.0)
                at = slice(128 * k, 128 * k + 128)
                asm[0, xp, :, at] = pltpu.roll(jnp.where(sub == 7, below, 0.0), 64, 1)
                asm[1, xp, :, at] = pltpu.roll(mid, 64, 1)
                asm[2, xp, :, at] = pltpu.roll(jnp.where(sub == 0, above, 0.0), 64, 1)
        for x_pos in range(3):
            src = ((0, 1), (1, 9), (9, 10))[x_pos]
            dst = ((56, 64), (0, 64), (0, 8))[x_pos]
            size = dst[1] - dst[0]
            low = lax.broadcasted_iota(jnp.int32, (size, 128), 1) < 64
            for y_pos in range(3):
                base = x_pos * 9 + y_pos * 3
                tiles = [
                    asm[y_pos, src[0] : src[1], :, 128 * k : 128 * k + 128].reshape(size, 128)
                    for k in range(5)
                ]
                before, mid, after = table[b, base], table[b, base + 1], table[b, base + 2]
                here = slice(dst[0], dst[1])
                gext[before, here, 384:512] += jnp.where(low, 0.0, tiles[0])
                for j in range(4):
                    at = slice(128 * j, 128 * j + 128)
                    gext[mid, here, at] += jnp.where(low, tiles[j], tiles[j + 1])
                gext[after, here, 0:128] += jnp.where(low, tiles[4], 0.0)
        return carry

    lax.fori_loop(0, count, spread_brick, 0)

    def give_own(b, carry):
        own[b] = gext[b]
        return carry

    def give_back(s, carry):
        ret[s] = gext[count + s].astype(BF16)
        return carry

    lax.fori_loop(0, count, give_own, 0)
    lax.fori_loop(0, slots, give_back, 0)


def last_kernel(scale, chosen, own, came, keepx, wsum, grad_features, grad_conv, grad_down, acc):
    count = keepx.shape[0]
    slots = came.shape[0]
    for b in range(count):
        acc[b] = own[b]
    acc[count] = jnp.zeros((64, 512), F32)

    def add(s, carry):
        to = chosen[s]
        acc[to] = acc[to] + came[s].astype(F32)
        return carry

    lax.fori_loop(0, slots, add, 0)
    for b in range(count):
        grad_features[b] = (acc[b] * keepx[b].astype(F32)).astype(BF16)
    decode(scale, wsum, grad_conv, grad_down)


def decode(scale, wsum, grad_conv, grad_down):
    grad_down[...] = wsum[896:1408, :].astype(F32) * scale
    for tap in range(9):
        first = (wsum[tap * 64 : tap * 64 + 64, :].astype(F32) * scale).T
        grad_conv[tap * 192 : tap * 192 + 128, :] = first
    for pair in range(5):
        lo = 576 + pair * 64
        both = (wsum[lo : lo + 64, :].astype(F32) * scale).T
        for part in range(2):
            tap = 2 * pair + part
            if tap < 9:
                at = tap * 192 + 128
                grad_conv[at : at + 64, :] = both[part * 64 : part * 64 + 64, :]


def call(kernel, shapes, in_spaces, scratch, args):
    spaces = {"s": pltpu.SMEM, "v": pltpu.VMEM, "a": pl.ANY}
    return pl.pallas_call(
        kernel,
        out_shape=[jax.ShapeDtypeStruct(shape, kind) for shape, kind in shapes],
        in_specs=[pl.BlockSpec(memory_space=spaces[s]) for s in in_spaces],
        out_specs=[pl.BlockSpec(memory_space=pltpu.VMEM) for _ in shapes],
        scratch_shapes=scratch,
        compiler_params=pltpu.CompilerParams(vmem_limit_bytes=VMEM_BYTES),
    )(*args)


def shards(features, masks, rulebook, send_lists, conv_weight, down_weight, cotangent):
    count = features.shape[1]
    peers = lax.axis_size("spatial")
    devices = peers * lax.axis_size("dp")
    cap = send_lists.shape[3]
    slots = peers * cap
    total = count + slots + 1
    rows = count * 256
    unit = devices * 16
    wrows = -(-1408 // unit) * unit
    scale = float(devices * count * 512) ** (-0.5)
    chosen = send_lists.reshape(slots)
    brick = (64, 512)
    masked, keepx, outgoing = call(
        first_kernel,
        [((count + 1, *brick), BF16), ((count, *brick), BF16), ((slots, *brick), BF16)],
        "svv",
        [],
        (chosen, features.reshape(count, *brick), masks[0]),
    )
    arrived = lax.all_to_all(
        outgoing.reshape(peers, cap, *brick), "spatial", split_axis=0, concat_axis=0, tiled=True
    ).reshape(slots, *brick)
    out, own, ret, wgrad = call(
        main_kernel,
        [
            ((count, 16, 512), BF16),
            ((count, *brick), F32),
            ((slots, *brick), BF16),
            ((wrows, 128), BF16),
        ],
        "saavvvv",
        [
            pltpu.VMEM((total, *brick), BF16),
            pltpu.VMEM((total, *brick), F32),
            pltpu.VMEM((rows, 2304), BF16),
            pltpu.VMEM((3, 10, 8, 640), F32),
            pltpu.VMEM((256, 2304), F32),
            pltpu.VMEM((rows, 128), F32),
            pltpu.VMEM((rows, 128), F32),
            pltpu.VMEM((rows, 128), F32),
            pltpu.VMEM((rows, 128), BF16),
            pltpu.VMEM((128, rows), BF16),
            pltpu.VMEM((2304, 128), BF16),
            pltpu.SemaphoreType.DMA((2,)),
        ],
        (
            rulebook[0],
            masked,
            arrived,
            keepx,
            conv_weight.reshape(27 * 64, 64),
            down_weight.reshape(512, 128),
            cotangent.reshape(count, 16, 512),
        ),
    )
    came = lax.all_to_all(
        ret.reshape(peers, cap, *brick), "spatial", split_axis=0, concat_axis=0, tiled=True
    ).reshape(slots, *brick)
    parts = lax.all_to_all(
        wgrad.reshape(devices, wrows // devices, 128),
        ("spatial", "dp"),
        split_axis=0,
        concat_axis=0,
        tiled=True,
    )
    mine = parts.astype(F32).sum(axis=0).astype(BF16)
    wsum = lax.all_gather(mine, ("spatial", "dp"), axis=0, tiled=True)
    grad_features, grad_conv, grad_down = call(
        functools.partial(last_kernel, scale),
        [((count, *brick), BF16), ((27 * 64, 64), F32), ((512, 128), F32)],
        "svvvv",
        [pltpu.VMEM((count + 1, *brick), F32)],
        (chosen, own, came, keepx, wsum),
    )
    return (
        out.reshape(1, count, 4, 4, 512),
        grad_features.reshape(features.shape),
        grad_conv.reshape(27, 64, 64),
        grad_down.reshape(8, 64, 128),
    )


def solution(mesh):
    placed = (
        P("dp", "spatial", None, None, None),
        P("dp", "spatial", None),
        P("dp", "spatial", None),
        P("dp", "spatial", None, None),
        P(),
        P(),
        P("dp", "spatial", None, None, None),
    )
    return jax.shard_map(
        shards,
        mesh=mesh,
        in_specs=placed,
        out_specs=(
            P("dp", "spatial", None, None, None),
            P("dp", "spatial", None, None, None),
            P(),
            P(),
        ),
        check_vma=False,
    )
```

```python
import functools

import jax
import jax.numpy as jnp
from jax import lax
from jax.experimental import pallas as pl
from jax.experimental.pallas import tpu as pltpu
from jax.sharding import PartitionSpec as P

F32 = jnp.float32
BF16 = jnp.bfloat16
VMEM_BYTES = 56 * 1024 * 1024


def silu_grad(value):
    sig = jax.nn.sigmoid(value)
    return sig * (1.0 + value * (1.0 - sig))


def first_kernel(chosen, feats, mask, masked, keepx, outgoing):
    count = feats.shape[0]
    slots = outgoing.shape[0]
    vox = lax.broadcasted_iota(jnp.int32, (64, 512), 1)
    row = lax.broadcasted_iota(jnp.int32, (64, 512), 0)
    own_row = (vox // 8) == row
    v_index = lax.broadcasted_iota(jnp.int32, (512, 512), 0)
    l_index = lax.broadcasted_iota(jnp.int32, (512, 512), 1)
    spread = ((v_index % 8) == (l_index // 64)).astype(F32).astype(BF16)
    for b in range(count):
        picked = jnp.where(own_row, mask[b : b + 1, :].astype(F32), 0.0).astype(BF16)
        keep = jnp.dot(picked, spread, preferred_element_type=F32)
        keepx[b] = keep.astype(BF16)
        masked[b] = (feats[b].astype(F32) * keep).astype(BF16)
    masked[count] = jnp.zeros((64, 512), BF16)

    def send(s, carry):
        outgoing[s] = masked[chosen[s]]
        return carry

    lax.fori_loop(0, slots, send, 0)


def main_kernel(
    table, masked, arrived, keepx, weight, down, cot,
    out, own, ret, wgrad,
    ext, gext, lhs, asm, dpad, pre, hid, keep, grad, grad_t, wpair, sems,
):
    count = keepx.shape[0]
    slots = arrived.shape[0]
    total = ext.shape[0]
    half_rows = count * 128
    rows = 2 * half_rows
    lane = lax.broadcasted_iota(jnp.int32, (8, 128), 1)

    fetch_own = pltpu.make_async_copy(masked.at[pl.ds(0, count)], ext.at[pl.ds(0, count)], sems.at[0])
    fetch_rest = pltpu.make_async_copy(arrived, ext.at[pl.ds(count, slots)], sems.at[1])
    fetch_own.start()
    fetch_rest.start()
    ext[total - 1] = jnp.zeros((64, 512), BF16)

    def clear(e, carry):
        gext[e] = jnp.zeros((64, 512), F32)
        return carry

    lax.fori_loop(0, total, clear, 0)

    for tap in range(9):
        taps = weight[tap * 192 : tap * 192 + 192, :].astype(F32)
        zero = jnp.zeros((64, 64), F32)
        left = jnp.concatenate([taps, zero], axis=0)
        right = jnp.concatenate([zero, taps], axis=0)
        wpair[tap * 256 : tap * 256 + 256, :] = jnp.concatenate([left, right], axis=1).astype(BF16)
    fetch_own.wait()
    fetch_rest.wait()

    def gather_brick(b, carry):
        for y_pos in range(3):
            for x_pos in range(3):
                src = ((48, 64), (0, 64), (0, 16))[x_pos]
                cut = ((8, 16), (0, 64), (0, 8))[x_pos]
                dst = ((0, 1), (1, 9), (9, 10))[x_pos]
                tiles = (dst[1] - dst[0], 8, 128)
                low = lax.broadcasted_iota(jnp.int32, tiles, 2) < 64
                base = x_pos * 9 + y_pos * 3

                def load(index, lo):
                    part = ext[index, src[0] : src[1], lo : lo + 128].astype(F32)
                    part = pltpu.roll(part[cut[0] : cut[1]], 64, 1)
                    return part.reshape(tiles)

                pieces = [load(table[b, base], 384)]
                mid = table[b, base + 1]
                for j in range(4):
                    pieces.append(load(mid, 128 * j))
                pieces.append(load(table[b, base + 2], 0))
                for k in range(5):
                    asm[y_pos, dst[0] : dst[1], :, 128 * k : 128 * k + 128] = jnp.where(
                        low, pieces[k], pieces[k + 1]
                    )
        sub = lax.broadcasted_iota(jnp.int32, (10, 8, 128), 1)
        for k in range(5):
            at = slice(128 * k, 128 * k + 128)
            mid = asm[1, :, :, at]
            below = pltpu.roll(jnp.where(sub == 7, asm[0, :, :, at], mid), 1, 1)
            above = pltpu.roll(jnp.where(sub == 0, asm[2, :, :, at], mid), 7, 1)
            for dy, value in enumerate((below, mid, above)):
                split = value.reshape(5, 2, 8, 128)
                for dx in range(3):
                    tap = dx * 3 + dy
                    for ox in range(2):
                        start, parity = (dx + ox) // 2, (dx + ox) % 2
                        block = split[start : start + 4, parity].reshape(32, 128).astype(BF16)
                        for p, part in ((k, 0), (k - 1, 1)):
                            if 0 <= p < 4:
                                at_row = pl.multiple_of(ox * half_rows + b * 128 + p * 32, 32)
                                col = tap * 256 + part * 128
                                lhs[pl.ds(at_row, 32), col : col + 128] = block
        spread = keepx[b].astype(F32).reshape(4, 2, 8, 512)
        for ox in range(2):
            for p in range(4):
                at_row = pl.multiple_of(ox * half_rows + b * 128 + p * 32, 32)
                keep[pl.ds(at_row, 32), :] = spread[:, ox, :, 128 * p : 128 * p + 128].reshape(32, 128)
        return carry

    lax.fori_loop(0, count, gather_brick, 0)

    def forward(i, carry):
        at = pl.ds(pl.multiple_of(i * 256, 256), 256)
        value = jnp.dot(lhs[at, :], wpair[...], preferred_element_type=F32) * keep[at, :]
        pre[at, :] = value
        hid[at, :] = value * jax.nn.sigmoid(value)
        return carry

    lax.fori_loop(0, count, forward, 0)

    coarse_rows = count * 64
    child = []
    summed = None
    coarse = None
    for o in range(4):
        at = pl.ds((o // 2) * half_rows + o % 2, coarse_rows, stride=2)
        child.append(hid[at, :].astype(BF16))
        term = jnp.dot(child[o], down[o * 128 : o * 128 + 128, :], preferred_element_type=F32)
        summed = term if o == 0 else summed + term
        active = keep[at, :]
        coarse = active if o == 0 else jnp.maximum(coarse, active)
    coarse = jnp.maximum(coarse, pltpu.roll(coarse, 64, 1))
    sig = jax.nn.sigmoid(summed)
    result = (summed * sig * coarse).astype(BF16)
    cots = []
    for b in range(count):
        for p in range(4):
            lo = (b * 4 + p) * 16
            out[b, :, 128 * p : 128 * p + 128] = result[lo : lo + 16, :]
            cots.append(cot[b, :, 128 * p : 128 * p + 128])
    upstream = jnp.concatenate(cots, axis=0).astype(F32)
    grad_pre = (upstream * coarse * (sig * (1.0 + summed * (1.0 - sig)))).astype(BF16)
    for o in range(4):
        part = lax.dot_general(
            child[o], grad_pre, (((0,), (0,)), ((), ())), preferred_element_type=F32
        )
        wgrad[896 + o * 128 : 896 + o * 128 + 128, :] = part.astype(BF16)
        back = lax.dot_general(
            grad_pre,
            down[o * 128 : o * 128 + 128, :],
            (((1,), (1,)), ((), ())),
            preferred_element_type=F32,
        )
        hid[pl.ds((o // 2) * half_rows + o % 2, coarse_rows, stride=2), :] = back
    if wgrad.shape[0] > 1408:
        wgrad[1408:, :] = jnp.zeros((wgrad.shape[0] - 1408, 128), BF16)

    def hidden_grad(i, carry):
        at = pl.ds(pl.multiple_of(i * 256, 256), 256)
        value = hid[at, :] * silu_grad(pre[at, :]) * keep[at, :]
        grad[at, :] = value.astype(BF16)
        grad_t[:, at] = value.T.astype(BF16)
        return carry

    lax.fori_loop(0, count, hidden_grad, 0)

    wide = lax.broadcasted_iota(jnp.int32, (64, 128), 1)
    spare = None
    for tap in range(9):
        both = jnp.dot(
            grad_t[...], lhs[:, tap * 256 : tap * 256 + 256], preferred_element_type=F32
        )
        sums = both[0:64, :] + pltpu.roll(both[64:128, :], 192, 1)
        wgrad[tap * 64 : tap * 64 + 64, :] = sums[:, 0:128].astype(BF16)
        last = sums[:, 128:256]
        if tap % 2 == 0:
            spare = last
        if tap % 2 == 1 or tap == 8:
            other = pltpu.roll(last, 64, 1) if tap % 2 == 1 else jnp.zeros_like(last)
            lo = 576 + (tap // 2) * 64
            wgrad[lo : lo + 64, :] = jnp.where(wide < 64, spare, other).astype(BF16)

    def spread_brick(b, carry):
        low_rows = pl.multiple_of(b * 128, 128)
        for ox in range(2):
            dpad[ox * 128 : ox * 128 + 128, :] = lax.dot_general(
                grad[pl.ds(ox * half_rows + low_rows, 128), :],
                wpair[...],
                (((1,), (1,)), ((), ())),
                preferred_element_type=F32,
            )
        sub = lax.broadcasted_iota(jnp.int32, (8, 128), 0)
        for xp in range(10):
            for k in range(5):
                acc = [None, None, None]
                for dy in range(3):
                    for dx in range(3):
                        x = xp - dx
                        if not 0 <= x < 8:
                            continue
                        for p, part in ((k, 0), (k - 1, 1)):
                            if 0 <= p < 4:
                                at_row = (x % 2) * 128 + p * 32 + (x // 2) * 8
                                col = (dx * 3 + dy) * 256 + part * 128
                                tile = dpad[at_row : at_row + 8, col : col + 128]
                                acc[dy] = tile if acc[dy] is None else acc[dy] + tile
                below = pltpu.roll(acc[0], 7, 0)
                above = pltpu.roll(acc[2], 1, 0)
                mid = acc[1] + jnp.where(sub < 7, below, 0.0) + jnp.where(sub > 0, above, 0.0)
                at = slice(128 * k, 128 * k + 128)
                asm[0, xp, :, at] = pltpu.roll(jnp.where(sub == 7, below, 0.0), 64, 1)
                asm[1, xp, :, at] = pltpu.roll(mid, 64, 1)
                asm[2, xp, :, at] = pltpu.roll(jnp.where(sub == 0, above, 0.0), 64, 1)
        for x_pos in range(3):
            src = ((0, 1), (1, 9), (9, 10))[x_pos]
            dst = ((56, 64), (0, 64), (0, 8))[x_pos]
            size = dst[1] - dst[0]
            low = lax.broadcasted_iota(jnp.int32, (size, 128), 1) < 64
            for y_pos in range(3):
                base = x_pos * 9 + y_pos * 3
                tiles = [
                    asm[y_pos, src[0] : src[1], :, 128 * k : 128 * k + 128].reshape(size, 128)
                    for k in range(5)
                ]
                before, mid, after = table[b, base], table[b, base + 1], table[b, base + 2]
                here = slice(dst[0], dst[1])
                gext[before, here, 384:512] += jnp.where(low, 0.0, tiles[0])
                for j in range(4):
                    at = slice(128 * j, 128 * j + 128)
                    gext[mid, here, at] += jnp.where(low, tiles[j], tiles[j + 1])
                gext[after, here, 0:128] += jnp.where(low, tiles[4], 0.0)
        return carry

    lax.fori_loop(0, count, spread_brick, 0)

    def give_own(b, carry):
        own[b] = gext[b]
        return carry

    def give_back(s, carry):
        ret[s] = gext[count + s].astype(BF16)
        return carry

    lax.fori_loop(0, count, give_own, 0)
    lax.fori_loop(0, slots, give_back, 0)


def region(d, edge):
    q = d // (edge * edge)
    return (q % 2 * (edge // 2) + q // 2, d // edge % edge, d % edge)


def relation(me, p, edge):
    apart = [jnp.abs(a - b) for a, b in zip(region(me, edge), region(p, edge))]
    near = jnp.maximum(jnp.maximum(apart[0], apart[1]), apart[2]) == 1
    face = apart[0] + apart[1] + apart[2] == 1
    return near, face


def halo_copies(me, peers, source, landed, send_sem, recv_sem, act):
    edge = round(peers ** (1 / 3))
    for p in range(peers):
        near, face = relation(me, p, edge)

        def run(cap, p=p):
            copy = pltpu.make_async_remote_copy(
                src_ref=source.at[p, pl.ds(0, cap)],
                dst_ref=landed.at[me, pl.ds(0, cap)],
                send_sem=send_sem.at[p],
                recv_sem=recv_sem.at[me],
                device_id={"spatial": p},
                device_id_type=pl.DeviceIdType.MESH,
            )
            back = pltpu.make_async_remote_copy(
                src_ref=source.at[p, pl.ds(0, cap)],
                dst_ref=landed.at[p, pl.ds(0, cap)],
                send_sem=send_sem.at[p],
                recv_sem=recv_sem.at[p],
                device_id={"spatial": p},
                device_id_type=pl.DeviceIdType.MESH,
            )
            act(copy, back)

        @pl.when(near & face)
        def _():
            run(2)

        @pl.when(near & jnp.logical_not(face))
        def _():
            run(1)


def start_copy(copy, back):
    copy.start()


def end_copy(copy, back):
    copy.wait_send()
    back.wait_recv()


def halo_kernel(peers, source, landed, send_sem, recv_sem):
    me = lax.axis_index("spatial")
    edge = round(peers ** (1 / 3))
    barrier = pltpu.get_barrier_semaphore()
    for p in range(peers):
        near, _ = relation(me, p, edge)

        @pl.when(near)
        def _():
            pl.semaphore_signal(
                barrier, inc=1, device_id={"spatial": p}, device_id_type=pl.DeviceIdType.MESH
            )

    number = sum(relation(me, p, edge)[0].astype(jnp.int32) for p in range(peers))
    pl.semaphore_wait(barrier, number)
    halo_copies(me, peers, source, landed, send_sem, recv_sem, start_copy)
    halo_copies(me, peers, source, landed, send_sem, recv_sem, end_copy)


def back_kernel(
    peers, groups, source, wgrad, landed, wsum,
    send_sem, recv_sem, group_in, group_sum, peer_in, peer_sum, gathered,
    gs_sem, gr_sem, ps_sem, pr_sem, as_sem, ar_sem, bs_sem, br_sem, own_sem,
):
    me = lax.axis_index("spatial")
    mine = lax.axis_index("dp")
    size = group_sum.shape[0]
    unit = peer_sum.shape[0]
    mesh = pl.DeviceIdType.MESH
    barrier = pltpu.get_barrier_semaphore()
    for k in range(1, peers):
        pl.semaphore_signal(
            barrier, inc=1, device_id={"spatial": (me + k) % peers}, device_id_type=mesh
        )
    for k in range(1, groups):
        pl.semaphore_signal(
            barrier, inc=1, device_id={"dp": (mine + k) % groups}, device_id_type=mesh
        )
    pl.semaphore_wait(barrier, peers + groups - 2)

    def group_copy(k):
        to = (mine + k) % groups
        return pltpu.make_async_remote_copy(
            src_ref=wgrad.at[pl.ds(to * size, size)],
            dst_ref=group_in.at[k - 1],
            send_sem=gs_sem.at[k - 1],
            recv_sem=gr_sem.at[k - 1],
            device_id={"dp": to},
            device_id_type=mesh,
        )

    def peer_copy(k):
        to = (me + k) % peers
        return pltpu.make_async_remote_copy(
            src_ref=group_sum.at[pl.ds(to * unit, unit)],
            dst_ref=peer_in.at[k - 1],
            send_sem=ps_sem.at[k - 1],
            recv_sem=pr_sem.at[k - 1],
            device_id={"spatial": to},
            device_id_type=mesh,
        )

    def gather_copy(k, owner):
        return pltpu.make_async_remote_copy(
            src_ref=peer_sum,
            dst_ref=gathered.at[pl.ds(owner * unit, unit)],
            send_sem=as_sem.at[k - 1],
            recv_sem=ar_sem.at[k - 1],
            device_id={"spatial": (me + k) % peers},
            device_id_type=mesh,
        )

    def spread_copy(k, owner):
        return pltpu.make_async_remote_copy(
            src_ref=gathered,
            dst_ref=wsum.at[pl.ds(owner * size, size)],
            send_sem=bs_sem.at[k - 1],
            recv_sem=br_sem.at[k - 1],
            device_id={"dp": (mine + k) % groups},
            device_id_type=mesh,
        )

    for k in range(1, groups):
        group_copy(k).start()
    halo_copies(me, peers, source, landed, send_sem, recv_sem, start_copy)
    total = wgrad[pl.ds(mine * size, size), :].astype(F32)
    for k in range(1, groups):
        group_copy(k).wait_recv()
        total = total + group_in[k - 1].astype(F32)
    group_sum[...] = total.astype(BF16)
    for k in range(1, peers):
        peer_copy(k).start()
    part = group_sum[pl.ds(me * unit, unit), :].astype(F32)
    for k in range(1, peers):
        peer_copy(k).wait_recv()
        part = part + peer_in[k - 1].astype(F32)
    peer_sum[...] = part.astype(BF16)
    for k in range(1, peers):
        gather_copy(k, me).start()
    gathered[pl.ds(me * unit, unit), :] = part.astype(BF16)
    for k in range(1, peers):
        gather_copy(k, (me + peers - k) % peers).wait_recv()
    own = pltpu.make_async_copy(gathered, wsum.at[pl.ds(mine * size, size)], own_sem)
    own.start()
    for k in range(1, groups):
        spread_copy(k, mine).start()
    for k in range(1, groups):
        spread_copy(k, (mine + groups - k) % groups).wait_recv()
    own.wait()
    for k in range(1, groups):
        group_copy(k).wait_send()
        spread_copy(k, mine).wait_send()
    for k in range(1, peers):
        peer_copy(k).wait_send()
        gather_copy(k, me).wait_send()
    halo_copies(me, peers, source, landed, send_sem, recv_sem, end_copy)


def last_kernel(scale, chosen, own, came, keepx, wsum, grad_features, grad_conv, grad_down, acc):
    count = keepx.shape[0]
    slots = came.shape[0]
    for b in range(count):
        acc[b] = own[b]
    acc[count] = jnp.zeros((64, 512), F32)

    def add(s, carry):
        to = chosen[s]
        acc[to] = acc[to] + came[s].astype(F32)
        return carry

    lax.fori_loop(0, slots, add, 0)
    for b in range(count):
        grad_features[b] = (acc[b] * keepx[b].astype(F32)).astype(BF16)
    decode(scale, wsum, grad_conv, grad_down)


def decode(scale, wsum, grad_conv, grad_down):
    grad_down[...] = wsum[896:1408, :].astype(F32) * scale
    for tap in range(9):
        first = (wsum[tap * 64 : tap * 64 + 64, :].astype(F32) * scale).T
        grad_conv[tap * 192 : tap * 192 + 128, :] = first
    for pair in range(5):
        lo = 576 + pair * 64
        both = (wsum[lo : lo + 64, :].astype(F32) * scale).T
        for part in range(2):
            tap = 2 * pair + part
            if tap < 9:
                at = tap * 192 + 128
                grad_conv[at : at + 64, :] = both[part * 64 : part * 64 + 64, :]


def call(kernel, shapes, in_spaces, scratch, args, collective=None):
    remote = collective is not None
    spaces = {"s": pltpu.SMEM, "v": pltpu.VMEM, "a": pl.ANY}
    return pl.pallas_call(
        kernel,
        out_shape=[jax.ShapeDtypeStruct(shape, kind) for shape, kind in shapes],
        in_specs=[pl.BlockSpec(memory_space=spaces[s]) for s in in_spaces],
        out_specs=[pl.BlockSpec(memory_space=pl.ANY if remote else pltpu.VMEM) for _ in shapes],
        scratch_shapes=scratch,
        compiler_params=pltpu.CompilerParams(
            vmem_limit_bytes=VMEM_BYTES, collective_id=collective, has_side_effects=remote
        ),
    )(*args)


def shards(features, masks, rulebook, send_lists, conv_weight, down_weight, cotangent):
    count = features.shape[1]
    peers = lax.axis_size("spatial")
    devices = peers * lax.axis_size("dp")
    cap = send_lists.shape[3]
    slots = peers * cap
    total = count + slots + 1
    rows = count * 256
    unit = devices * 16
    wrows = -(-1408 // unit) * unit
    scale = float(devices * count * 512) ** (-0.5)
    chosen = send_lists.reshape(slots)
    brick = (64, 512)
    masked, keepx, outgoing = call(
        first_kernel,
        [((count + 1, *brick), BF16), ((count, *brick), BF16), ((slots, *brick), BF16)],
        "svv",
        [],
        (chosen, features.reshape(count, *brick), masks[0]),
    )
    sems = [pltpu.SemaphoreType.DMA((peers,)), pltpu.SemaphoreType.DMA((peers,))]
    (arrived,) = call(
        functools.partial(halo_kernel, peers),
        [((peers, cap, *brick), BF16)],
        "a",
        sems,
        (outgoing.reshape(peers, cap, *brick),),
        collective=0,
    )
    arrived = arrived.reshape(slots, *brick)
    out, own, ret, wgrad = call(
        main_kernel,
        [
            ((count, 16, 512), BF16),
            ((count, *brick), F32),
            ((slots, *brick), BF16),
            ((wrows, 128), BF16),
        ],
        "saavvvv",
        [
            pltpu.VMEM((total, *brick), BF16),
            pltpu.VMEM((total, *brick), F32),
            pltpu.VMEM((rows, 2304), BF16),
            pltpu.VMEM((3, 10, 8, 640), F32),
            pltpu.VMEM((256, 2304), F32),
            pltpu.VMEM((rows, 128), F32),
            pltpu.VMEM((rows, 128), F32),
            pltpu.VMEM((rows, 128), F32),
            pltpu.VMEM((rows, 128), BF16),
            pltpu.VMEM((128, rows), BF16),
            pltpu.VMEM((2304, 128), BF16),
            pltpu.SemaphoreType.DMA((2,)),
        ],
        (
            rulebook[0],
            masked,
            arrived,
            keepx,
            conv_weight.reshape(27 * 64, 64),
            down_weight.reshape(512, 128),
            cotangent.reshape(count, 16, 512),
        ),
    )
    groups = devices // peers
    size = wrows // groups
    unit = wrows // devices
    came, wsum = call(
        functools.partial(back_kernel, peers, groups),
        [((peers, cap, *brick), BF16), ((wrows, 128), BF16)],
        "av",
        sems
        + [
            pltpu.VMEM((groups - 1, size, 128), BF16),
            pltpu.VMEM((size, 128), BF16),
            pltpu.VMEM((peers - 1, unit, 128), BF16),
            pltpu.VMEM((unit, 128), BF16),
            pltpu.VMEM((size, 128), BF16),
        ]
        + [pltpu.SemaphoreType.DMA((groups - 1,))] * 2
        + [pltpu.SemaphoreType.DMA((peers - 1,))] * 4
        + [pltpu.SemaphoreType.DMA((groups - 1,))] * 2
        + [pltpu.SemaphoreType.DMA],
        (ret.reshape(peers, cap, *brick), wgrad),
        collective=1,
    )
    came = came.reshape(slots, *brick)
    grad_features, grad_conv, grad_down = call(
        functools.partial(last_kernel, scale),
        [((count, *brick), BF16), ((27 * 64, 64), F32), ((512, 128), F32)],
        "svvvv",
        [pltpu.VMEM((count + 1, *brick), F32)],
        (chosen, own, came, keepx, wsum),
    )
    return (
        out.reshape(1, count, 4, 4, 512),
        grad_features.reshape(features.shape),
        grad_conv.reshape(27, 64, 64),
        grad_down.reshape(8, 64, 128),
    )


def solution(mesh):
    placed = (
        P("dp", "spatial", None, None, None),
        P("dp", "spatial", None),
        P("dp", "spatial", None),
        P("dp", "spatial", None, None),
        P(),
        P(),
        P("dp", "spatial", None, None, None),
    )
    return jax.shard_map(
        shards,
        mesh=mesh,
        in_specs=placed,
        out_specs=(
            P("dp", "spatial", None, None, None),
            P("dp", "spatial", None, None, None),
            P(),
            P(),
        ),
        check_vma=False,
    )
```

```python
import functools

import jax
import jax.numpy as jnp
from jax import lax
from jax.experimental import pallas as pl
from jax.experimental.pallas import tpu as pltpu
from jax.sharding import PartitionSpec as P

F32 = jnp.float32
BF16 = jnp.bfloat16
VMEM_BYTES = 56 * 1024 * 1024


def silu_grad(value):
    sig = jax.nn.sigmoid(value)
    return sig * (1.0 + value * (1.0 - sig))


def pack(value, stage):
    for k in range(4):
        stage[k] = value[:, 128 * k : 128 * k + 128]
    tiles = [stage[k, 0:8, :] for k in range(4)]
    tiles += [stage[k, 56:64, :] for k in range(4)]
    tiles += [stage[k, pl.ds(0, 8, stride=8), :] for k in range(4)]
    tiles += [stage[k, pl.ds(7, 8, stride=8), :] for k in range(4)]
    low = lax.broadcasted_iota(jnp.int32, (48, 128), 1) < 64
    tiles.append(jnp.where(low, stage[0, 8:56, :], stage[3, 8:56, :]))
    return jnp.concatenate(tiles, axis=0).astype(BF16)


def unpack(rim, stage):
    value = rim.astype(F32)
    low = lax.broadcasted_iota(jnp.int32, (48, 128), 1) < 64
    stage[0, 8:56, :] = jnp.where(low, value[128:176], 0.0)
    stage[3, 8:56, :] = jnp.where(low, 0.0, value[128:176])
    for k in range(4):
        stage[k, pl.ds(0, 8, stride=8), :] = value[64 + 8 * k : 72 + 8 * k]
        stage[k, pl.ds(7, 8, stride=8), :] = value[96 + 8 * k : 104 + 8 * k]
        stage[k, 0:8, :] = value[8 * k : 8 * k + 8]
        stage[k, 56:64, :] = value[32 + 8 * k : 40 + 8 * k]


def first_kernel(chosen, feats, mask, masked, keepx, outgoing, work, rims):
    count = feats.shape[0]
    slots = outgoing.shape[0]
    vox = lax.broadcasted_iota(jnp.int32, (64, 512), 1)
    row = lax.broadcasted_iota(jnp.int32, (64, 512), 0)
    own_row = (vox // 8) == row
    v_index = lax.broadcasted_iota(jnp.int32, (512, 512), 0)
    l_index = lax.broadcasted_iota(jnp.int32, (512, 512), 1)
    spread = ((v_index % 8) == (l_index // 64)).astype(F32).astype(BF16)
    for b in range(count):
        picked = jnp.where(own_row, mask[b : b + 1, :].astype(F32), 0.0).astype(BF16)
        keep = jnp.dot(picked, spread, preferred_element_type=F32)
        keepx[b] = keep.astype(BF16)
        value = feats[b].astype(F32) * keep
        masked[b] = value.astype(BF16)
        rims[b] = pack(value, work.at[b])
    rims[count] = jnp.zeros((176, 128), BF16)

    def send(s, carry):
        outgoing[s] = rims[chosen[s]]
        return carry

    lax.fori_loop(0, slots, send, 0)


def main_kernel(
    table, masked, arrived, keepx, weight, down, cot,
    out, own, ret, wgrad,
    ext, gext, lhs, asm, dpad, pre, hid, keep, grad, grad_t, wpair, work, sems,
):
    count = keepx.shape[0]
    slots = arrived.shape[0]
    total = ext.shape[0]
    half_rows = count * 128
    rows = 2 * half_rows
    lane = lax.broadcasted_iota(jnp.int32, (8, 128), 1)

    fetch_own = pltpu.make_async_copy(masked, ext.at[pl.ds(0, count)], sems.at[0])
    fetch_own.start()
    work[...] = jnp.zeros((4, 64, 128), F32)

    def put_arrived(s, carry):
        unpack(arrived[s], work)
        for k in range(4):
            ext[count + s, :, 128 * k : 128 * k + 128] = work[k].astype(BF16)
        return carry

    lax.fori_loop(0, slots, put_arrived, 0)
    ext[total - 1] = jnp.zeros((64, 512), BF16)

    def clear(e, carry):
        gext[e] = jnp.zeros((64, 512), F32)
        return carry

    lax.fori_loop(0, total, clear, 0)

    for tap in range(9):
        taps = weight[tap * 192 : tap * 192 + 192, :].astype(F32)
        zero = jnp.zeros((64, 64), F32)
        left = jnp.concatenate([taps, zero], axis=0)
        right = jnp.concatenate([zero, taps], axis=0)
        wpair[tap * 256 : tap * 256 + 256, :] = jnp.concatenate([left, right], axis=1).astype(BF16)
    fetch_own.wait()

    def gather_brick(b, carry):
        for y_pos in range(3):
            for x_pos in range(3):
                src = ((48, 64), (0, 64), (0, 16))[x_pos]
                cut = ((8, 16), (0, 64), (0, 8))[x_pos]
                dst = ((0, 1), (1, 9), (9, 10))[x_pos]
                tiles = (dst[1] - dst[0], 8, 128)
                low = lax.broadcasted_iota(jnp.int32, tiles, 2) < 64
                base = x_pos * 9 + y_pos * 3

                def load(index, lo):
                    part = ext[index, src[0] : src[1], lo : lo + 128].astype(F32)
                    part = pltpu.roll(part[cut[0] : cut[1]], 64, 1)
                    return part.reshape(tiles)

                pieces = [load(table[b, base], 384)]
                mid = table[b, base + 1]
                for j in range(4):
                    pieces.append(load(mid, 128 * j))
                pieces.append(load(table[b, base + 2], 0))
                for k in range(5):
                    asm[y_pos, dst[0] : dst[1], :, 128 * k : 128 * k + 128] = jnp.where(
                        low, pieces[k], pieces[k + 1]
                    )
        sub = lax.broadcasted_iota(jnp.int32, (10, 8, 128), 1)
        for k in range(5):
            at = slice(128 * k, 128 * k + 128)
            mid = asm[1, :, :, at]
            below = pltpu.roll(jnp.where(sub == 7, asm[0, :, :, at], mid), 1, 1)
            above = pltpu.roll(jnp.where(sub == 0, asm[2, :, :, at], mid), 7, 1)
            for dy, value in enumerate((below, mid, above)):
                split = value.reshape(5, 2, 8, 128)
                for dx in range(3):
                    tap = dx * 3 + dy
                    for ox in range(2):
                        start, parity = (dx + ox) // 2, (dx + ox) % 2
                        block = split[start : start + 4, parity].reshape(32, 128).astype(BF16)
                        for p, part in ((k, 0), (k - 1, 1)):
                            if 0 <= p < 4:
                                at_row = pl.multiple_of(ox * half_rows + b * 128 + p * 32, 32)
                                col = tap * 256 + part * 128
                                lhs[pl.ds(at_row, 32), col : col + 128] = block
        spread = keepx[b].astype(F32).reshape(4, 2, 8, 512)
        for ox in range(2):
            for p in range(4):
                at_row = pl.multiple_of(ox * half_rows + b * 128 + p * 32, 32)
                keep[pl.ds(at_row, 32), :] = spread[:, ox, :, 128 * p : 128 * p + 128].reshape(32, 128)
        return carry

    lax.fori_loop(0, count, gather_brick, 0)

    def forward(i, carry):
        at = pl.ds(pl.multiple_of(i * 256, 256), 256)
        value = jnp.dot(lhs[at, :], wpair[...], preferred_element_type=F32) * keep[at, :]
        pre[at, :] = value
        hid[at, :] = value * jax.nn.sigmoid(value)
        return carry

    lax.fori_loop(0, count, forward, 0)

    coarse_rows = count * 64
    child = []
    summed = None
    coarse = None
    for o in range(4):
        at = pl.ds((o // 2) * half_rows + o % 2, coarse_rows, stride=2)
        child.append(hid[at, :].astype(BF16))
        term = jnp.dot(child[o], down[o * 128 : o * 128 + 128, :], preferred_element_type=F32)
        summed = term if o == 0 else summed + term
        active = keep[at, :]
        coarse = active if o == 0 else jnp.maximum(coarse, active)
    coarse = jnp.maximum(coarse, pltpu.roll(coarse, 64, 1))
    sig = jax.nn.sigmoid(summed)
    result = (summed * sig * coarse).astype(BF16)
    cots = []
    for b in range(count):
        for p in range(4):
            lo = (b * 4 + p) * 16
            out[b, :, 128 * p : 128 * p + 128] = result[lo : lo + 16, :]
            cots.append(cot[b, :, 128 * p : 128 * p + 128])
    upstream = jnp.concatenate(cots, axis=0).astype(F32)
    grad_pre = (upstream * coarse * (sig * (1.0 + summed * (1.0 - sig)))).astype(BF16)
    for o in range(4):
        part = lax.dot_general(
            child[o], grad_pre, (((0,), (0,)), ((), ())), preferred_element_type=F32
        )
        wgrad[896 + o * 128 : 896 + o * 128 + 128, :] = part.astype(BF16)
        back = lax.dot_general(
            grad_pre,
            down[o * 128 : o * 128 + 128, :],
            (((1,), (1,)), ((), ())),
            preferred_element_type=F32,
        )
        hid[pl.ds((o // 2) * half_rows + o % 2, coarse_rows, stride=2), :] = back
    if wgrad.shape[0] > 1408:
        wgrad[1408:, :] = jnp.zeros((wgrad.shape[0] - 1408, 128), BF16)

    def hidden_grad(i, carry):
        at = pl.ds(pl.multiple_of(i * 256, 256), 256)
        value = hid[at, :] * silu_grad(pre[at, :]) * keep[at, :]
        grad[at, :] = value.astype(BF16)
        grad_t[:, at] = value.T.astype(BF16)
        return carry

    lax.fori_loop(0, count, hidden_grad, 0)

    wide = lax.broadcasted_iota(jnp.int32, (64, 128), 1)
    spare = None
    for tap in range(9):
        both = jnp.dot(
            grad_t[...], lhs[:, tap * 256 : tap * 256 + 256], preferred_element_type=F32
        )
        sums = both[0:64, :] + pltpu.roll(both[64:128, :], 192, 1)
        wgrad[tap * 64 : tap * 64 + 64, :] = sums[:, 0:128].astype(BF16)
        last = sums[:, 128:256]
        if tap % 2 == 0:
            spare = last
        if tap % 2 == 1 or tap == 8:
            other = pltpu.roll(last, 64, 1) if tap % 2 == 1 else jnp.zeros_like(last)
            lo = 576 + (tap // 2) * 64
            wgrad[lo : lo + 64, :] = jnp.where(wide < 64, spare, other).astype(BF16)

    def spread_brick(b, carry):
        low_rows = pl.multiple_of(b * 128, 128)
        for ox in range(2):
            dpad[ox * 128 : ox * 128 + 128, :] = lax.dot_general(
                grad[pl.ds(ox * half_rows + low_rows, 128), :],
                wpair[...],
                (((1,), (1,)), ((), ())),
                preferred_element_type=F32,
            )
        sub = lax.broadcasted_iota(jnp.int32, (8, 128), 0)
        for xp in range(10):
            for k in range(5):
                acc = [None, None, None]
                for dy in range(3):
                    for dx in range(3):
                        x = xp - dx
                        if not 0 <= x < 8:
                            continue
                        for p, part in ((k, 0), (k - 1, 1)):
                            if 0 <= p < 4:
                                at_row = (x % 2) * 128 + p * 32 + (x // 2) * 8
                                col = (dx * 3 + dy) * 256 + part * 128
                                tile = dpad[at_row : at_row + 8, col : col + 128]
                                acc[dy] = tile if acc[dy] is None else acc[dy] + tile
                below = pltpu.roll(acc[0], 7, 0)
                above = pltpu.roll(acc[2], 1, 0)
                mid = acc[1] + jnp.where(sub < 7, below, 0.0) + jnp.where(sub > 0, above, 0.0)
                at = slice(128 * k, 128 * k + 128)
                asm[0, xp, :, at] = pltpu.roll(jnp.where(sub == 7, below, 0.0), 64, 1)
                asm[1, xp, :, at] = pltpu.roll(mid, 64, 1)
                asm[2, xp, :, at] = pltpu.roll(jnp.where(sub == 0, above, 0.0), 64, 1)
        for x_pos in range(3):
            src = ((0, 1), (1, 9), (9, 10))[x_pos]
            dst = ((56, 64), (0, 64), (0, 8))[x_pos]
            size = dst[1] - dst[0]
            low = lax.broadcasted_iota(jnp.int32, (size, 128), 1) < 64
            for y_pos in range(3):
                base = x_pos * 9 + y_pos * 3
                tiles = [
                    asm[y_pos, src[0] : src[1], :, 128 * k : 128 * k + 128].reshape(size, 128)
                    for k in range(5)
                ]
                before, mid, after = table[b, base], table[b, base + 1], table[b, base + 2]
                here = slice(dst[0], dst[1])
                gext[before, here, 384:512] += jnp.where(low, 0.0, tiles[0])
                for j in range(4):
                    at = slice(128 * j, 128 * j + 128)
                    gext[mid, here, at] += jnp.where(low, tiles[j], tiles[j + 1])
                gext[after, here, 0:128] += jnp.where(low, tiles[4], 0.0)
        return carry

    lax.fori_loop(0, count, spread_brick, 0)

    def give_own(b, carry):
        own[b] = gext[b]
        return carry

    def give_back(s, carry):
        ret[s] = pack(gext[count + s], work)
        return carry

    lax.fori_loop(0, count, give_own, 0)
    lax.fori_loop(0, slots, give_back, 0)


def region(d, edge):
    q = d // (edge * edge)
    return (q % 2 * (edge // 2) + q // 2, d // edge % edge, d % edge)


def relation(me, p, edge):
    apart = [jnp.abs(a - b) for a, b in zip(region(me, edge), region(p, edge))]
    near = jnp.maximum(jnp.maximum(apart[0], apart[1]), apart[2]) == 1
    face = apart[0] + apart[1] + apart[2] == 1
    return near, face


def halo_copies(me, peers, source, landed, send_sem, recv_sem, act, faces=True, others=True):
    edge = round(peers ** (1 / 3))
    for p in range(peers):
        near, face = relation(me, p, edge)

        def run(cap, p=p):
            copy = pltpu.make_async_remote_copy(
                src_ref=source.at[p, pl.ds(0, cap)],
                dst_ref=landed.at[me, pl.ds(0, cap)],
                send_sem=send_sem.at[p],
                recv_sem=recv_sem.at[me],
                device_id={"spatial": p},
                device_id_type=pl.DeviceIdType.MESH,
            )
            back = pltpu.make_async_remote_copy(
                src_ref=source.at[p, pl.ds(0, cap)],
                dst_ref=landed.at[p, pl.ds(0, cap)],
                send_sem=send_sem.at[p],
                recv_sem=recv_sem.at[p],
                device_id={"spatial": p},
                device_id_type=pl.DeviceIdType.MESH,
            )
            act(copy, back)

        if faces:

            @pl.when(near & face)
            def _():
                run(2)

        if others:

            @pl.when(near & jnp.logical_not(face))
            def _():
                run(1)


def start_copy(copy, back):
    copy.start()


def end_copy(copy, back):
    copy.wait_send()
    back.wait_recv()


def halo_kernel(peers, source, landed, send_sem, recv_sem):
    me = lax.axis_index("spatial")
    edge = round(peers ** (1 / 3))
    barrier = pltpu.get_barrier_semaphore()
    for p in range(peers):
        near, _ = relation(me, p, edge)

        @pl.when(near)
        def _():
            pl.semaphore_signal(
                barrier, inc=1, device_id={"spatial": p}, device_id_type=pl.DeviceIdType.MESH
            )

    number = sum(relation(me, p, edge)[0].astype(jnp.int32) for p in range(peers))
    pl.semaphore_wait(barrier, number)
    halo_copies(me, peers, source, landed, send_sem, recv_sem, start_copy)
    halo_copies(me, peers, source, landed, send_sem, recv_sem, end_copy)


def back_kernel(
    peers, groups, source, wgrad, landed, wsum,
    send_sem, recv_sem, group_in, group_sum, peer_in, peer_sum, gathered,
    gs_sem, gr_sem, ps_sem, pr_sem, as_sem, ar_sem, bs_sem, br_sem, own_sem,
):
    me = lax.axis_index("spatial")
    mine = lax.axis_index("dp")
    size = group_sum.shape[0]
    unit = peer_sum.shape[0]
    mesh = pl.DeviceIdType.MESH
    barrier = pltpu.get_barrier_semaphore()
    for k in range(1, peers):
        pl.semaphore_signal(
            barrier, inc=1, device_id={"spatial": (me + k) % peers}, device_id_type=mesh
        )
    for k in range(1, groups):
        pl.semaphore_signal(
            barrier, inc=1, device_id={"dp": (mine + k) % groups}, device_id_type=mesh
        )
    pl.semaphore_wait(barrier, peers + groups - 2)

    def group_copy(k):
        to = (mine + k) % groups
        return pltpu.make_async_remote_copy(
            src_ref=wgrad.at[pl.ds(to * size, size)],
            dst_ref=group_in.at[k - 1],
            send_sem=gs_sem.at[k - 1],
            recv_sem=gr_sem.at[k - 1],
            device_id={"dp": to},
            device_id_type=mesh,
        )

    def peer_copy(k):
        to = (me + k) % peers
        return pltpu.make_async_remote_copy(
            src_ref=group_sum.at[pl.ds(to * unit, unit)],
            dst_ref=peer_in.at[k - 1],
            send_sem=ps_sem.at[k - 1],
            recv_sem=pr_sem.at[k - 1],
            device_id={"spatial": to},
            device_id_type=mesh,
        )

    def gather_copy(k, owner):
        return pltpu.make_async_remote_copy(
            src_ref=peer_sum,
            dst_ref=gathered.at[pl.ds(owner * unit, unit)],
            send_sem=as_sem.at[k - 1],
            recv_sem=ar_sem.at[k - 1],
            device_id={"spatial": (me + k) % peers},
            device_id_type=mesh,
        )

    def spread_copy(k, owner):
        return pltpu.make_async_remote_copy(
            src_ref=gathered,
            dst_ref=wsum.at[pl.ds(owner * size, size)],
            send_sem=bs_sem.at[k - 1],
            recv_sem=br_sem.at[k - 1],
            device_id={"dp": (mine + k) % groups},
            device_id_type=mesh,
        )

    for k in range(1, groups):
        group_copy(k).start()
    halo_copies(me, peers, source, landed, send_sem, recv_sem, start_copy, others=False)
    total = wgrad[pl.ds(mine * size, size), :].astype(F32)
    for k in range(1, groups):
        group_copy(k).wait_recv()
        total = total + group_in[k - 1].astype(F32)
    group_sum[...] = total.astype(BF16)
    for k in range(1, peers):
        peer_copy(k).start()
    part = group_sum[pl.ds(me * unit, unit), :].astype(F32)
    for k in range(1, peers):
        peer_copy(k).wait_recv()
        part = part + peer_in[k - 1].astype(F32)
    peer_sum[...] = part.astype(BF16)
    for k in range(1, peers):
        gather_copy(k, me).start()
    halo_copies(me, peers, source, landed, send_sem, recv_sem, start_copy, faces=False)
    gathered[pl.ds(me * unit, unit), :] = part.astype(BF16)
    for k in range(1, peers):
        gather_copy(k, (me + peers - k) % peers).wait_recv()
    own = pltpu.make_async_copy(gathered, wsum.at[pl.ds(mine * size, size)], own_sem)
    own.start()
    for k in range(1, groups):
        spread_copy(k, mine).start()
    for k in range(1, groups):
        spread_copy(k, (mine + groups - k) % groups).wait_recv()
    own.wait()
    for k in range(1, groups):
        group_copy(k).wait_send()
        spread_copy(k, mine).wait_send()
    for k in range(1, peers):
        peer_copy(k).wait_send()
        gather_copy(k, me).wait_send()
    halo_copies(me, peers, source, landed, send_sem, recv_sem, end_copy)


def last_kernel(scale, chosen, own, came, keepx, wsum, grad_features, grad_conv, grad_down, acc, work):
    count = keepx.shape[0]
    slots = came.shape[0]
    for b in range(count):
        acc[b] = own[b]
    acc[count] = jnp.zeros((64, 512), F32)
    work[...] = jnp.zeros((4, 64, 128), F32)

    def add(s, carry):
        to = chosen[s]
        unpack(came[s], work)
        for k in range(4):
            acc[to, :, 128 * k : 128 * k + 128] += work[k]
        return carry

    lax.fori_loop(0, slots, add, 0)
    for b in range(count):
        grad_features[b] = (acc[b] * keepx[b].astype(F32)).astype(BF16)
    decode(scale, wsum, grad_conv, grad_down)


def decode(scale, wsum, grad_conv, grad_down):
    grad_down[...] = wsum[896:1408, :].astype(F32) * scale
    for tap in range(9):
        first = (wsum[tap * 64 : tap * 64 + 64, :].astype(F32) * scale).T
        grad_conv[tap * 192 : tap * 192 + 128, :] = first
    for pair in range(5):
        lo = 576 + pair * 64
        both = (wsum[lo : lo + 64, :].astype(F32) * scale).T
        for part in range(2):
            tap = 2 * pair + part
            if tap < 9:
                at = tap * 192 + 128
                grad_conv[at : at + 64, :] = both[part * 64 : part * 64 + 64, :]


def call(kernel, shapes, in_spaces, scratch, args, collective=None):
    remote = collective is not None
    spaces = {"s": pltpu.SMEM, "v": pltpu.VMEM, "a": pl.ANY}
    return pl.pallas_call(
        kernel,
        out_shape=[jax.ShapeDtypeStruct(shape, kind) for shape, kind in shapes],
        in_specs=[pl.BlockSpec(memory_space=spaces[s]) for s in in_spaces],
        out_specs=[pl.BlockSpec(memory_space=pl.ANY if remote else pltpu.VMEM) for _ in shapes],
        scratch_shapes=scratch,
        compiler_params=pltpu.CompilerParams(
            vmem_limit_bytes=VMEM_BYTES, collective_id=collective, has_side_effects=remote
        ),
    )(*args)


def shards(features, masks, rulebook, send_lists, conv_weight, down_weight, cotangent):
    count = features.shape[1]
    peers = lax.axis_size("spatial")
    devices = peers * lax.axis_size("dp")
    cap = send_lists.shape[3]
    slots = peers * cap
    total = count + slots + 1
    rows = count * 256
    unit = devices * 16
    wrows = -(-1408 // unit) * unit
    scale = float(devices * count * 512) ** (-0.5)
    chosen = send_lists.reshape(slots)
    brick = (64, 512)
    rim = (176, 128)
    masked, keepx, outgoing = call(
        first_kernel,
        [((count, *brick), BF16), ((count, *brick), BF16), ((slots, *rim), BF16)],
        "svv",
        [pltpu.VMEM((count, 4, 64, 128), F32), pltpu.VMEM((count + 1, *rim), BF16)],
        (chosen, features.reshape(count, *brick), masks[0]),
    )
    sems = [pltpu.SemaphoreType.DMA((peers,)), pltpu.SemaphoreType.DMA((peers,))]
    (arrived,) = call(
        functools.partial(halo_kernel, peers),
        [((peers, cap, *rim), BF16)],
        "a",
        sems,
        (outgoing.reshape(peers, cap, *rim),),
        collective=0,
    )
    arrived = arrived.reshape(slots, *rim)
    out, own, ret, wgrad = call(
        main_kernel,
        [
            ((count, 16, 512), BF16),
            ((count, *brick), F32),
            ((slots, *rim), BF16),
            ((wrows, 128), BF16),
        ],
        "savvvvv",
        [
            pltpu.VMEM((total, *brick), BF16),
            pltpu.VMEM((total, *brick), F32),
            pltpu.VMEM((rows, 2304), BF16),
            pltpu.VMEM((3, 10, 8, 640), F32),
            pltpu.VMEM((256, 2304), F32),
            pltpu.VMEM((rows, 128), F32),
            pltpu.VMEM((rows, 128), F32),
            pltpu.VMEM((rows, 128), F32),
            pltpu.VMEM((rows, 128), BF16),
            pltpu.VMEM((128, rows), BF16),
            pltpu.VMEM((2304, 128), BF16),
            pltpu.VMEM((4, 64, 128), F32),
            pltpu.SemaphoreType.DMA((1,)),
        ],
        (
            rulebook[0],
            masked,
            arrived,
            keepx,
            conv_weight.reshape(27 * 64, 64),
            down_weight.reshape(512, 128),
            cotangent.reshape(count, 16, 512),
        ),
    )
    groups = devices // peers
    size = wrows // groups
    unit = wrows // devices
    came, wsum = call(
        functools.partial(back_kernel, peers, groups),
        [((peers, cap, *rim), BF16), ((wrows, 128), BF16)],
        "av",
        sems
        + [
            pltpu.VMEM((groups - 1, size, 128), BF16),
            pltpu.VMEM((size, 128), BF16),
            pltpu.VMEM((peers - 1, unit, 128), BF16),
            pltpu.VMEM((unit, 128), BF16),
            pltpu.VMEM((size, 128), BF16),
        ]
        + [pltpu.SemaphoreType.DMA((groups - 1,))] * 2
        + [pltpu.SemaphoreType.DMA((peers - 1,))] * 4
        + [pltpu.SemaphoreType.DMA((groups - 1,))] * 2
        + [pltpu.SemaphoreType.DMA],
        (ret.reshape(peers, cap, *rim), wgrad),
        collective=1,
    )
    came = came.reshape(slots, *rim)
    grad_features, grad_conv, grad_down = call(
        functools.partial(last_kernel, scale),
        [((count, *brick), BF16), ((27 * 64, 64), F32), ((512, 128), F32)],
        "svvvv",
        [pltpu.VMEM((count + 1, *brick), F32), pltpu.VMEM((4, 64, 128), F32)],
        (chosen, own, came, keepx, wsum),
    )
    return (
        out.reshape(1, count, 4, 4, 512),
        grad_features.reshape(features.shape),
        grad_conv.reshape(27, 64, 64),
        grad_down.reshape(8, 64, 128),
    )


def solution(mesh):
    placed = (
        P("dp", "spatial", None, None, None),
        P("dp", "spatial", None),
        P("dp", "spatial", None),
        P("dp", "spatial", None, None),
        P(),
        P(),
        P("dp", "spatial", None, None, None),
    )
    return jax.shard_map(
        shards,
        mesh=mesh,
        in_specs=placed,
        out_specs=(
            P("dp", "spatial", None, None, None),
            P("dp", "spatial", None, None, None),
            P(),
            P(),
        ),
        check_vma=False,
    )
```

```python
import functools

import jax
import jax.numpy as jnp
from jax import lax
from jax.experimental import pallas as pl
from jax.experimental.pallas import tpu as pltpu
from jax.sharding import PartitionSpec as P

F32 = jnp.float32
BF16 = jnp.bfloat16
VMEM_BYTES = 56 * 1024 * 1024


def silu_grad(value):
    sig = jax.nn.sigmoid(value)
    return sig * (1.0 + value * (1.0 - sig))


def pack(value, stage):
    for k in range(4):
        stage[k] = value[:, 128 * k : 128 * k + 128]
    tiles = [stage[k, 0:8, :] for k in range(4)]
    tiles += [stage[k, 56:64, :] for k in range(4)]
    tiles += [stage[k, pl.ds(0, 8, stride=8), :] for k in range(4)]
    tiles += [stage[k, pl.ds(7, 8, stride=8), :] for k in range(4)]
    low = lax.broadcasted_iota(jnp.int32, (48, 128), 1) < 64
    tiles.append(jnp.where(low, stage[0, 8:56, :], stage[3, 8:56, :]))
    return jnp.concatenate(tiles, axis=0).astype(BF16)


def unpack(rim, stage):
    value = rim.astype(F32)
    low = lax.broadcasted_iota(jnp.int32, (48, 128), 1) < 64
    stage[0, 8:56, :] = jnp.where(low, value[128:176], 0.0)
    stage[3, 8:56, :] = jnp.where(low, 0.0, value[128:176])
    for k in range(4):
        stage[k, pl.ds(0, 8, stride=8), :] = value[64 + 8 * k : 72 + 8 * k]
        stage[k, pl.ds(7, 8, stride=8), :] = value[96 + 8 * k : 104 + 8 * k]
        stage[k, 0:8, :] = value[8 * k : 8 * k + 8]
        stage[k, 56:64, :] = value[32 + 8 * k : 40 + 8 * k]


def first_kernel(chosen, feats, mask, masked, keepx, outgoing, work, rims):
    count = feats.shape[0]
    slots = outgoing.shape[0]
    cap = chosen.shape[0]
    vox = lax.broadcasted_iota(jnp.int32, (64, 512), 1)
    row = lax.broadcasted_iota(jnp.int32, (64, 512), 0)
    own_row = (vox // 8) == row
    v_index = lax.broadcasted_iota(jnp.int32, (512, 512), 0)
    l_index = lax.broadcasted_iota(jnp.int32, (512, 512), 1)
    spread = ((v_index % 8) == (l_index // 64)).astype(F32).astype(BF16)
    for b in range(count):
        picked = jnp.where(own_row, mask[b].astype(F32), 0.0).astype(BF16)
        keep = jnp.dot(picked, spread, preferred_element_type=F32)
        keepx[b] = keep.astype(BF16)
        value = feats[b].astype(F32) * keep
        masked[b] = value.astype(BF16)
        rims[b] = pack(value, work.at[b])
    rims[count] = jnp.zeros((176, 128), BF16)

    def send(s, carry):
        outgoing[s] = rims[chosen[s % cap, s // cap]]
        return carry

    lax.fori_loop(0, slots, send, 0)


def main_kernel(
    table, masked, arrived, keepx, weight, down, cot,
    out, own, ret, wgrad,
    ext, gext, lhs, asm, dpad, pre, hid, keep, grad, grad_t, wpair, work, coarse_work, sems,
):
    count = keepx.shape[0]
    slots = arrived.shape[0]
    total = ext.shape[0]
    half_rows = count * 128
    rows = 2 * half_rows
    lane = lax.broadcasted_iota(jnp.int32, (8, 128), 1)

    fetch_own = pltpu.make_async_copy(masked, ext.at[pl.ds(0, count)], sems.at[0])
    fetch_own.start()
    work[...] = jnp.zeros((4, 64, 128), F32)

    def put_arrived(s, carry):
        unpack(arrived[s], work)
        for k in range(4):
            ext[count + s, :, 128 * k : 128 * k + 128] = work[k].astype(BF16)
        return carry

    lax.fori_loop(0, slots, put_arrived, 0)
    ext[total - 1] = jnp.zeros((64, 512), BF16)

    def clear(e, carry):
        gext[e] = jnp.zeros((64, 512), F32)
        return carry

    lax.fori_loop(0, total, clear, 0)

    for tap in range(9):
        taps = weight[tap * 192 : tap * 192 + 192, :].astype(F32)
        zero = jnp.zeros((64, 64), F32)
        left = jnp.concatenate([taps, zero], axis=0)
        right = jnp.concatenate([zero, taps], axis=0)
        wpair[tap * 256 : tap * 256 + 256, :] = jnp.concatenate([left, right], axis=1).astype(BF16)
    fetch_own.wait()

    def gather_brick(b, carry):
        for y_pos in range(3):
            for x_pos in range(3):
                src = ((48, 64), (0, 64), (0, 16))[x_pos]
                cut = ((8, 16), (0, 64), (0, 8))[x_pos]
                dst = ((0, 1), (1, 9), (9, 10))[x_pos]
                tiles = (dst[1] - dst[0], 8, 128)
                low = lax.broadcasted_iota(jnp.int32, tiles, 2) < 64
                base = x_pos * 9 + y_pos * 3

                def load(index, lo):
                    part = ext[index, src[0] : src[1], lo : lo + 128].astype(F32)
                    part = pltpu.roll(part[cut[0] : cut[1]], 64, 1)
                    return part.reshape(tiles)

                pieces = [load(table[b, 0, base], 384)]
                mid = table[b, 0, base + 1]
                for j in range(4):
                    pieces.append(load(mid, 128 * j))
                pieces.append(load(table[b, 0, base + 2], 0))
                for k in range(5):
                    asm[y_pos, dst[0] : dst[1], :, 128 * k : 128 * k + 128] = jnp.where(
                        low, pieces[k], pieces[k + 1]
                    )
        sub = lax.broadcasted_iota(jnp.int32, (10, 8, 128), 1)
        for k in range(5):
            at = slice(128 * k, 128 * k + 128)
            mid = asm[1, :, :, at]
            below = pltpu.roll(jnp.where(sub == 7, asm[0, :, :, at], mid), 1, 1)
            above = pltpu.roll(jnp.where(sub == 0, asm[2, :, :, at], mid), 7, 1)
            for dy, value in enumerate((below, mid, above)):
                split = value.reshape(5, 2, 8, 128)
                for dx in range(3):
                    tap = dx * 3 + dy
                    for ox in range(2):
                        start, parity = (dx + ox) // 2, (dx + ox) % 2
                        block = split[start : start + 4, parity].reshape(32, 128).astype(BF16)
                        for p, part in ((k, 0), (k - 1, 1)):
                            if 0 <= p < 4:
                                at_row = pl.multiple_of(ox * half_rows + b * 128 + p * 32, 32)
                                col = tap * 256 + part * 128
                                lhs[pl.ds(at_row, 32), col : col + 128] = block
        spread = keepx[b].astype(F32).reshape(4, 2, 8, 512)
        for ox in range(2):
            for p in range(4):
                at_row = pl.multiple_of(ox * half_rows + b * 128 + p * 32, 32)
                keep[pl.ds(at_row, 32), :] = spread[:, ox, :, 128 * p : 128 * p + 128].reshape(32, 128)
        return carry

    lax.fori_loop(0, count, gather_brick, 0)

    def forward(i, carry):
        at = pl.ds(pl.multiple_of(i * 256, 256), 256)
        value = jnp.dot(lhs[at, :], wpair[...], preferred_element_type=F32) * keep[at, :]
        pre[at, :] = value
        hid[at, :] = value * jax.nn.sigmoid(value)
        return carry

    lax.fori_loop(0, count, forward, 0)

    coarse_rows = count * 64
    child = []
    summed = None
    coarse = None
    for o in range(4):
        at = pl.ds((o // 2) * half_rows + o % 2, coarse_rows, stride=2)
        child.append(hid[at, :].astype(BF16))
        term = jnp.dot(child[o], down[o * 128 : o * 128 + 128, :], preferred_element_type=F32)
        summed = term if o == 0 else summed + term
        active = keep[at, :]
        coarse = active if o == 0 else jnp.maximum(coarse, active)
    coarse = jnp.maximum(coarse, pltpu.roll(coarse, 64, 1))
    sig = jax.nn.sigmoid(summed)
    coarse_work[...] = summed * sig * coarse
    for b in range(count):
        for p in range(4):
            for x in range(4):
                lo = (b * 4 + p) * 16 + x * 4
                at = slice(128 * p, 128 * p + 128)
                out[b * 4 + x, :, at] = coarse_work[lo : lo + 4, :].astype(BF16)
    for b in range(count):
        for p in range(4):
            for x in range(4):
                lo = (b * 4 + p) * 16 + x * 4
                at = slice(128 * p, 128 * p + 128)
                coarse_work[lo : lo + 4, :] = cot[b * 4 + x, :, at].astype(F32)
    upstream = coarse_work[...]
    grad_pre = (upstream * coarse * (sig * (1.0 + summed * (1.0 - sig)))).astype(BF16)
    for o in range(4):
        part = lax.dot_general(
            child[o], grad_pre, (((0,), (0,)), ((), ())), preferred_element_type=F32
        )
        wgrad[896 + o * 128 : 896 + o * 128 + 128, :] = part.astype(BF16)
        back = lax.dot_general(
            grad_pre,
            down[o * 128 : o * 128 + 128, :],
            (((1,), (1,)), ((), ())),
            preferred_element_type=F32,
        )
        hid[pl.ds((o // 2) * half_rows + o % 2, coarse_rows, stride=2), :] = back
    if wgrad.shape[0] > 1408:
        wgrad[1408:, :] = jnp.zeros((wgrad.shape[0] - 1408, 128), BF16)

    def hidden_grad(i, carry):
        at = pl.ds(pl.multiple_of(i * 256, 256), 256)
        value = hid[at, :] * silu_grad(pre[at, :]) * keep[at, :]
        grad[at, :] = value.astype(BF16)
        grad_t[:, at] = value.T.astype(BF16)
        return carry

    lax.fori_loop(0, count, hidden_grad, 0)

    wide = lax.broadcasted_iota(jnp.int32, (64, 128), 1)
    spare = None
    for tap in range(9):
        both = jnp.dot(
            grad_t[...], lhs[:, tap * 256 : tap * 256 + 256], preferred_element_type=F32
        )
        sums = both[0:64, :] + pltpu.roll(both[64:128, :], 192, 1)
        wgrad[tap * 64 : tap * 64 + 64, :] = sums[:, 0:128].astype(BF16)
        last = sums[:, 128:256]
        if tap % 2 == 0:
            spare = last
        if tap % 2 == 1 or tap == 8:
            other = pltpu.roll(last, 64, 1) if tap % 2 == 1 else jnp.zeros_like(last)
            lo = 576 + (tap // 2) * 64
            wgrad[lo : lo + 64, :] = jnp.where(wide < 64, spare, other).astype(BF16)

    def spread_brick(b, carry):
        low_rows = pl.multiple_of(b * 128, 128)
        for ox in range(2):
            dpad[ox * 128 : ox * 128 + 128, :] = lax.dot_general(
                grad[pl.ds(ox * half_rows + low_rows, 128), :],
                wpair[...],
                (((1,), (1,)), ((), ())),
                preferred_element_type=F32,
            )
        sub = lax.broadcasted_iota(jnp.int32, (8, 128), 0)
        for xp in range(10):
            for k in range(5):
                acc = [None, None, None]
                for dy in range(3):
                    for dx in range(3):
                        x = xp - dx
                        if not 0 <= x < 8:
                            continue
                        for p, part in ((k, 0), (k - 1, 1)):
                            if 0 <= p < 4:
                                at_row = (x % 2) * 128 + p * 32 + (x // 2) * 8
                                col = (dx * 3 + dy) * 256 + part * 128
                                tile = dpad[at_row : at_row + 8, col : col + 128]
                                acc[dy] = tile if acc[dy] is None else acc[dy] + tile
                below = pltpu.roll(acc[0], 7, 0)
                above = pltpu.roll(acc[2], 1, 0)
                mid = acc[1] + jnp.where(sub < 7, below, 0.0) + jnp.where(sub > 0, above, 0.0)
                at = slice(128 * k, 128 * k + 128)
                asm[0, xp, :, at] = pltpu.roll(jnp.where(sub == 7, below, 0.0), 64, 1)
                asm[1, xp, :, at] = pltpu.roll(mid, 64, 1)
                asm[2, xp, :, at] = pltpu.roll(jnp.where(sub == 0, above, 0.0), 64, 1)
        for x_pos in range(3):
            src = ((0, 1), (1, 9), (9, 10))[x_pos]
            dst = ((56, 64), (0, 64), (0, 8))[x_pos]
            size = dst[1] - dst[0]
            low = lax.broadcasted_iota(jnp.int32, (size, 128), 1) < 64
            for y_pos in range(3):
                base = x_pos * 9 + y_pos * 3
                tiles = [
                    asm[y_pos, src[0] : src[1], :, 128 * k : 128 * k + 128].reshape(size, 128)
                    for k in range(5)
                ]
                before, mid, after = table[b, 0, base], table[b, 0, base + 1], table[b, 0, base + 2]
                here = slice(dst[0], dst[1])
                gext[before, here, 384:512] += jnp.where(low, 0.0, tiles[0])
                for j in range(4):
                    at = slice(128 * j, 128 * j + 128)
                    gext[mid, here, at] += jnp.where(low, tiles[j], tiles[j + 1])
                gext[after, here, 0:128] += jnp.where(low, tiles[4], 0.0)
        return carry

    lax.fori_loop(0, count, spread_brick, 0)

    def give_own(b, carry):
        own[b] = gext[b]
        return carry

    def give_back(s, carry):
        ret[s] = pack(gext[count + s], work)
        return carry

    lax.fori_loop(0, count, give_own, 0)
    lax.fori_loop(0, slots, give_back, 0)


def region(d, edge):
    q = d // (edge * edge)
    return (q % 2 * (edge // 2) + q // 2, d // edge % edge, d % edge)


def relation(me, p, edge):
    apart = [jnp.abs(a - b) for a, b in zip(region(me, edge), region(p, edge))]
    near = jnp.maximum(jnp.maximum(apart[0], apart[1]), apart[2]) == 1
    face = apart[0] + apart[1] + apart[2] == 1
    return near, face


def halo_copies(me, peers, source, landed, send_sem, recv_sem, act, faces=True, others=True):
    edge = round(peers ** (1 / 3))
    for p in range(peers):
        near, face = relation(me, p, edge)

        def run(cap, p=p):
            copy = pltpu.make_async_remote_copy(
                src_ref=source.at[p, pl.ds(0, cap)],
                dst_ref=landed.at[me, pl.ds(0, cap)],
                send_sem=send_sem.at[p],
                recv_sem=recv_sem.at[me],
                device_id={"spatial": p},
                device_id_type=pl.DeviceIdType.MESH,
            )
            back = pltpu.make_async_remote_copy(
                src_ref=source.at[p, pl.ds(0, cap)],
                dst_ref=landed.at[p, pl.ds(0, cap)],
                send_sem=send_sem.at[p],
                recv_sem=recv_sem.at[p],
                device_id={"spatial": p},
                device_id_type=pl.DeviceIdType.MESH,
            )
            act(copy, back)

        if faces:

            @pl.when(near & face)
            def _():
                run(2)

        if others:

            @pl.when(near & jnp.logical_not(face))
            def _():
                run(1)


def start_copy(copy, back):
    copy.start()


def end_copy(copy, back):
    copy.wait_send()
    back.wait_recv()


def halo_kernel(peers, source, landed, send_sem, recv_sem):
    me = lax.axis_index("spatial")
    edge = round(peers ** (1 / 3))
    barrier = pltpu.get_barrier_semaphore()
    for p in range(peers):
        near, _ = relation(me, p, edge)

        @pl.when(near)
        def _():
            pl.semaphore_signal(
                barrier, inc=1, device_id={"spatial": p}, device_id_type=pl.DeviceIdType.MESH
            )

    number = sum(relation(me, p, edge)[0].astype(jnp.int32) for p in range(peers))
    pl.semaphore_wait(barrier, number)
    halo_copies(me, peers, source, landed, send_sem, recv_sem, start_copy)
    halo_copies(me, peers, source, landed, send_sem, recv_sem, end_copy)


def back_kernel(
    peers, groups, source, wgrad, landed, wsum,
    send_sem, recv_sem, group_in, group_sum, peer_in, peer_sum, gathered,
    gs_sem, gr_sem, ps_sem, pr_sem, as_sem, ar_sem, bs_sem, br_sem, own_sem,
):
    me = lax.axis_index("spatial")
    mine = lax.axis_index("dp")
    size = group_sum.shape[0]
    unit = peer_sum.shape[0]
    mesh = pl.DeviceIdType.MESH
    barrier = pltpu.get_barrier_semaphore()
    for k in range(1, peers):
        pl.semaphore_signal(
            barrier, inc=1, device_id={"spatial": (me + k) % peers}, device_id_type=mesh
        )
    for k in range(1, groups):
        pl.semaphore_signal(
            barrier, inc=1, device_id={"dp": (mine + k) % groups}, device_id_type=mesh
        )
    pl.semaphore_wait(barrier, peers + groups - 2)

    def group_copy(k):
        to = (mine + k) % groups
        return pltpu.make_async_remote_copy(
            src_ref=wgrad.at[pl.ds(to * size, size)],
            dst_ref=group_in.at[k - 1],
            send_sem=gs_sem.at[k - 1],
            recv_sem=gr_sem.at[k - 1],
            device_id={"dp": to},
            device_id_type=mesh,
        )

    def peer_copy(k):
        to = (me + k) % peers
        return pltpu.make_async_remote_copy(
            src_ref=group_sum.at[pl.ds(to * unit, unit)],
            dst_ref=peer_in.at[k - 1],
            send_sem=ps_sem.at[k - 1],
            recv_sem=pr_sem.at[k - 1],
            device_id={"spatial": to},
            device_id_type=mesh,
        )

    def gather_copy(k, owner):
        return pltpu.make_async_remote_copy(
            src_ref=peer_sum,
            dst_ref=gathered.at[pl.ds(owner * unit, unit)],
            send_sem=as_sem.at[k - 1],
            recv_sem=ar_sem.at[k - 1],
            device_id={"spatial": (me + k) % peers},
            device_id_type=mesh,
        )

    def spread_copy(k, owner):
        return pltpu.make_async_remote_copy(
            src_ref=gathered,
            dst_ref=wsum.at[pl.ds(owner * size, size)],
            send_sem=bs_sem.at[k - 1],
            recv_sem=br_sem.at[k - 1],
            device_id={"dp": (mine + k) % groups},
            device_id_type=mesh,
        )

    for k in range(1, groups):
        group_copy(k).start()
    halo_copies(me, peers, source, landed, send_sem, recv_sem, start_copy, others=False)
    total = wgrad[pl.ds(mine * size, size), :].astype(F32)
    for k in range(1, groups):
        group_copy(k).wait_recv()
        total = total + group_in[k - 1].astype(F32)
    group_sum[...] = total.astype(BF16)
    for k in range(1, peers):
        peer_copy(k).start()
    part = group_sum[pl.ds(me * unit, unit), :].astype(F32)
    for k in range(1, peers):
        peer_copy(k).wait_recv()
        part = part + peer_in[k - 1].astype(F32)
    peer_sum[...] = part.astype(BF16)
    for k in range(1, peers):
        gather_copy(k, me).start()
    halo_copies(me, peers, source, landed, send_sem, recv_sem, start_copy, faces=False)
    gathered[pl.ds(me * unit, unit), :] = part.astype(BF16)
    for k in range(1, peers):
        gather_copy(k, (me + peers - k) % peers).wait_recv()
    own = pltpu.make_async_copy(gathered, wsum.at[pl.ds(mine * size, size)], own_sem)
    own.start()
    for k in range(1, groups):
        spread_copy(k, mine).start()
    for k in range(1, groups):
        spread_copy(k, (mine + groups - k) % groups).wait_recv()
    own.wait()
    for k in range(1, groups):
        group_copy(k).wait_send()
        spread_copy(k, mine).wait_send()
    for k in range(1, peers):
        peer_copy(k).wait_send()
        gather_copy(k, me).wait_send()
    halo_copies(me, peers, source, landed, send_sem, recv_sem, end_copy)


def last_kernel(scale, chosen, own, came, keepx, wsum, grad_features, grad_conv, grad_down, acc, work):
    count = keepx.shape[0]
    slots = came.shape[0]
    cap = chosen.shape[0]
    for b in range(count):
        acc[b] = own[b]
    acc[count] = jnp.zeros((64, 512), F32)
    work[...] = jnp.zeros((4, 64, 128), F32)

    def add(s, carry):
        to = chosen[s % cap, s // cap]
        unpack(came[s], work)
        for k in range(4):
            acc[to, :, 128 * k : 128 * k + 128] += work[k]
        return carry

    lax.fori_loop(0, slots, add, 0)
    for b in range(count):
        grad_features[b] = (acc[b] * keepx[b].astype(F32)).astype(BF16)
    decode(scale, wsum, grad_conv, grad_down)


def decode(scale, wsum, grad_conv, grad_down):
    grad_down[...] = wsum[896:1408, :].astype(F32) * scale
    for tap in range(9):
        first = (wsum[tap * 64 : tap * 64 + 64, :].astype(F32) * scale).T
        grad_conv[tap * 192 : tap * 192 + 128, :] = first
    for pair in range(5):
        lo = 576 + pair * 64
        both = (wsum[lo : lo + 64, :].astype(F32) * scale).T
        for part in range(2):
            tap = 2 * pair + part
            if tap < 9:
                at = tap * 192 + 128
                grad_conv[at : at + 64, :] = both[part * 64 : part * 64 + 64, :]


def call(kernel, shapes, in_spaces, scratch, args, collective=None):
    remote = collective is not None
    spaces = {"s": pltpu.SMEM, "v": pltpu.VMEM, "a": pl.ANY}
    return pl.pallas_call(
        kernel,
        out_shape=[jax.ShapeDtypeStruct(shape, kind) for shape, kind in shapes],
        in_specs=[pl.BlockSpec(memory_space=spaces[s]) for s in in_spaces],
        out_specs=[pl.BlockSpec(memory_space=pl.ANY if remote else pltpu.VMEM) for _ in shapes],
        scratch_shapes=scratch,
        compiler_params=pltpu.CompilerParams(
            vmem_limit_bytes=VMEM_BYTES, collective_id=collective, has_side_effects=remote
        ),
    )(*args)


def shards(features, masks, rulebook, send_lists, conv_weight, down_weight, cotangent):
    count = features.shape[1]
    peers = lax.axis_size("spatial")
    devices = peers * lax.axis_size("dp")
    cap = send_lists.shape[3]
    slots = peers * cap
    total = count + slots + 1
    rows = count * 256
    unit = devices * 16
    wrows = -(-1408 // unit) * unit
    scale = float(devices * count * 512) ** (-0.5)
    chosen = send_lists[0, 0].T
    brick = (64, 512)
    rim = (176, 128)
    masked, keepx, outgoing = call(
        first_kernel,
        [((count, *brick), BF16), ((count, *brick), BF16), ((slots, *rim), BF16)],
        "svv",
        [pltpu.VMEM((count, 4, 64, 128), F32), pltpu.VMEM((count + 1, *rim), BF16)],
        (chosen, features.reshape(count, *brick), masks.reshape(count, 1, 512)),
    )
    sems = [pltpu.SemaphoreType.DMA((peers,)), pltpu.SemaphoreType.DMA((peers,))]
    (arrived,) = call(
        functools.partial(halo_kernel, peers),
        [((peers, cap, *rim), BF16)],
        "a",
        sems,
        (outgoing.reshape(peers, cap, *rim),),
        collective=0,
    )
    arrived = arrived.reshape(slots, *rim)
    out, own, ret, wgrad = call(
        main_kernel,
        [
            ((count * 4, 4, 512), BF16),
            ((count, *brick), F32),
            ((slots, *rim), BF16),
            ((wrows, 128), BF16),
        ],
        "savvvvv",
        [
            pltpu.VMEM((total, *brick), BF16),
            pltpu.VMEM((total, *brick), F32),
            pltpu.VMEM((rows, 2304), BF16),
            pltpu.VMEM((3, 10, 8, 640), F32),
            pltpu.VMEM((256, 2304), F32),
            pltpu.VMEM((rows, 128), F32),
            pltpu.VMEM((rows, 128), F32),
            pltpu.VMEM((rows, 128), F32),
            pltpu.VMEM((rows, 128), BF16),
            pltpu.VMEM((128, rows), BF16),
            pltpu.VMEM((2304, 128), BF16),
            pltpu.VMEM((4, 64, 128), F32),
            pltpu.VMEM((count * 64, 128), F32),
            pltpu.SemaphoreType.DMA((1,)),
        ],
        (
            rulebook.reshape(count, 1, 27),
            masked,
            arrived,
            keepx,
            conv_weight.reshape(27 * 64, 64),
            down_weight.reshape(512, 128),
            cotangent.reshape(count * 4, 4, 512),
        ),
    )
    groups = devices // peers
    size = wrows // groups
    unit = wrows // devices
    came, wsum = call(
        functools.partial(back_kernel, peers, groups),
        [((peers, cap, *rim), BF16), ((wrows, 128), BF16)],
        "av",
        sems
        + [
            pltpu.VMEM((groups - 1, size, 128), BF16),
            pltpu.VMEM((size, 128), BF16),
            pltpu.VMEM((peers - 1, unit, 128), BF16),
            pltpu.VMEM((unit, 128), BF16),
            pltpu.VMEM((size, 128), BF16),
        ]
        + [pltpu.SemaphoreType.DMA((groups - 1,))] * 2
        + [pltpu.SemaphoreType.DMA((peers - 1,))] * 4
        + [pltpu.SemaphoreType.DMA((groups - 1,))] * 2
        + [pltpu.SemaphoreType.DMA],
        (ret.reshape(peers, cap, *rim), wgrad),
        collective=1,
    )
    came = came.reshape(slots, *rim)
    grad_features, grad_conv, grad_down = call(
        functools.partial(last_kernel, scale),
        [((count, *brick), BF16), ((27 * 64, 64), F32), ((512, 128), F32)],
        "svvvv",
        [pltpu.VMEM((count + 1, *brick), F32), pltpu.VMEM((4, 64, 128), F32)],
        (chosen, own, came, keepx, wsum),
    )
    return (
        out.reshape(1, count, 4, 4, 512),
        grad_features.reshape(features.shape),
        grad_conv.reshape(27, 64, 64),
        grad_down.reshape(8, 64, 128),
    )


def solution(mesh):
    placed = (
        P("dp", "spatial", None, None, None),
        P("dp", "spatial", None),
        P("dp", "spatial", None),
        P("dp", "spatial", None, None),
        P(),
        P(),
        P("dp", "spatial", None, None, None),
    )
    return jax.shard_map(
        shards,
        mesh=mesh,
        in_specs=placed,
        out_specs=(
            P("dp", "spatial", None, None, None),
            P("dp", "spatial", None, None, None),
            P(),
            P(),
        ),
        check_vma=False,
    )
```
